32 devices in a mesh: rows: 4 (over z), cols: 4 (over y, core), rep: 2 (over x).
Axes of the slice: x: 2, y: 2, z: 4, core: 2. Of those that a mesh axis runs over, the one named last changes fastest.
Arguments:
- inputs: bfloat16 [8, 64, 128, 256], P('rep', 'rows', 'cols'), may hold values from -6 to 6
- upstream: bfloat16 [8, 64, 128, 256], P('rep', 'rows', 'cols'), may hold values from -6 to 6
- kernel: bfloat16 [3, 3, 256, 256], replicated, may hold values from -0.125 to 0.125
- probe_init: float32 [64, 128, 256], P('rows', 'cols'), may hold values from -18 to 18
Outputs:
- outputs: bfloat16 [8, 64, 128, 256], P('rep', 'rows', 'cols')
- input_grad: bfloat16 [8, 64, 128, 256], P('rep', 'rows', 'cols')
- kernel_grad: float32 [256, 2304], P(('rows', 'cols'))
- probe_out: float32 [64, 128, 256], P('rows', 'cols')
- lipschitz: float32 [], replicated
- norm_trace: float32 [3], replicated
The draws below stay inside these ranges and needn't reach their ends.
All inputs are finite; a program needn't handle non-finite values.
Results may differ from the reference program's by a relative error of at most 0.011.
Values may be sent and summed in bfloat16 or wider, within the bound.
A program may use at most 128 MiB of HBM per device.

```python
import jax
import jax.numpy as jnp

C = 256
ITERS = 4
NH = 64
NW = 128
BATCH = 8


def draw_probe_init(key, part):
    ramp = jnp.arange(NH, dtype=jnp.float32) / max(NH - 1, 1)
    row_scale = 1.0 + 2.0 * ramp
    sample = jax.random.normal(key, (NH, NW, C), jnp.float32)
    return jnp.clip(sample * row_scale[:, None, None], -18.0, 18.0)


def raised(result, key, source, target, shards_of, factor):
    owner, partner = [(jnp.arange(result.shape[dim]) // (result.shape[dim] // shards_of)).reshape([-1 if axis == dim else 1 for axis in range(result.ndim)]) for dim in (source, target)]
    chosen = jax.random.permutation(key, shards_of)[partner]
    strong = (owner == chosen) | (owner == (partner + shards_of // 2) % shards_of)
    return jnp.where(strong, factor * result, result)


def block_levels(rng, shape, split, least, largest):
    gain = 1.0
    for dim, parts in split:
        heights = jax.random.uniform(jax.random.fold_in(jax.random.fold_in(rng, 6), dim), (parts,), jnp.float32, least / len(split), largest / len(split))
        gain = gain * jnp.repeat(jnp.exp(heights), shape[dim] // parts).reshape((-1,) + (1,) * (len(shape) - 1 - dim))
    return gain


def scatter_about(own_key, extent, deviation, reach, cuts=(), held_as=jnp.bfloat16):
    entries = jax.random.normal(own_key, extent, jnp.float32) * deviation
    if len(cuts) > 0:
        entries = block_levels(own_key, extent, cuts, -0.22, 0.18) * entries
    return jnp.clip(entries, min=-reach, max=reach).astype(held_as)


def gaussian_with(key, shape, scale, most, shards, heavy, held_as=jnp.bfloat16):
    result = scale * jax.random.normal(key, shape, jnp.float32)
    if shards:
        result = result * block_levels(key, shape, shards, -0.22, 0.18)
    return jnp.clip(raised(result, jax.random.fold_in(key, 3), *heavy), -most, most).astype(held_as)


def setup_inputs(seed: int = 0) -> dict:
    arg_keys = jax.random.split(jax.random.key(seed), 5)
    return {
        "inputs": scatter_about(arg_keys[0], (BATCH, NH, NW, C), 1.0, 6.0, ((0, 2), (1, 4), (2, 4))),
        "upstream": gaussian_with(arg_keys[1], (BATCH, NH, NW, C), 1.0, 6.0, ((0, 2), (1, 4), (2, 4)), (1, 3, 4, 2.0)),
        "kernel": scatter_about(arg_keys[2], (3, 3, C, C), (9 * C) ** -0.5, 0.125),
        "probe_init": draw_probe_init(jax.random.fold_in(arg_keys[4], 71), 0),
    }


def spatial_pad(field, periodic):
    widths = [(0, 0)] * (field.ndim - 3) + [(1, 1), (1, 1), (0, 0)]
    if periodic:
        return jnp.pad(field, widths, mode='wrap')
    return jnp.pad(field, widths)

def tap_sum(padded, kernel, height, breadth, adjoint):
    summed = None
    for row_tap in range(3):
        for col_tap in range(3):
            weights = kernel[row_tap, col_tap].astype(jnp.float32)
            if adjoint:
                window = padded[..., 2 - row_tap:2 - row_tap + height, 2 - col_tap:2 - col_tap + breadth, :]
                contrib = jnp.einsum('...d,cd->...c', window.astype(jnp.float32), weights)
            else:
                window = padded[..., row_tap:row_tap + height, col_tap:col_tap + breadth, :]
                contrib = jnp.einsum('...c,cd->...d', window.astype(jnp.float32), weights)
            summed = contrib if summed is None else summed + contrib
    return summed

def reference(inputs, upstream, kernel, probe_init):
    count = NH * NW * C
    iterate = probe_init.astype(jnp.bfloat16)
    back = None
    traces = []
    for iteration in range(ITERS):
        image = tap_sum(spatial_pad(iterate, True), kernel, NH, NW, False).astype(jnp.bfloat16)
        back = tap_sum(spatial_pad(image, True), kernel, NH, NW, True)
        if iteration + 1 < ITERS:
            scale_now = jnp.sqrt(jnp.sum(back * back) / count + 1e-06)
            traces.append(scale_now)
            iterate = (back / scale_now).astype(jnp.bfloat16)
    norm_trace = jnp.stack(traces).astype(jnp.float32)
    sum_back = jnp.sum(back * back)
    wide_iter = iterate.astype(jnp.float32)
    sum_probe = jnp.sum(wide_iter * wide_iter)
    lipschitz = jnp.sqrt(jnp.sqrt(sum_back / sum_probe))
    probe_out = back / jnp.sqrt(sum_back / count + 1e-06)
    padded_in = spatial_pad(inputs, False)
    outputs = tap_sum(padded_in, kernel, NH, NW, False).astype(jnp.bfloat16)
    input_grad = tap_sum(spatial_pad(upstream, False), kernel, NH, NW, True).astype(jnp.bfloat16)
    wide_up = upstream.astype(jnp.float32)
    pieces = []
    for row_tap in range(3):
        for col_tap in range(3):
            window = padded_in[:, row_tap:row_tap + NH, col_tap:col_tap + NW, :].astype(jnp.float32)
            pieces.append(jnp.einsum('nhwd,nhwc->dc', wide_up, window))
    stacked = jnp.stack(pieces, axis=1).reshape(C, 9 * C)
    kernel_grad = stacked * (1.0 / jnp.sqrt(jnp.float32(BATCH * NH * NW)))
    return (outputs, input_grad, kernel_grad, probe_out, lipschitz, norm_trace)
```

```python
import functools
import math

import jax
import jax.numpy as jnp
from jax import lax
from jax.experimental import pallas as pl
from jax.experimental.pallas import tpu as pltpu
from jax.sharding import PartitionSpec as P

MESH = pl.DeviceIdType.MESH
ITERS = 4
F32 = jnp.float32
BF16 = jnp.bfloat16
SIDES = [(v, h) for v in (-1, 0, 1) for h in (-1, 0, 1) if (v, h) != (0, 0)]


def split_rows(rows):
    for block in (13, 11, 10, 9, 8, 7, 6, 5, 4, 3, 2):
        if rows % block == 0:
            return block
    return 1


def kernel(
    nr, nc, counts, in_ref, up_ref, k_ref, p_ref,
    o_ref, g_ref, kg_ref, po_ref, sc_ref,
    fs_row, fr_row, fs_col, fr_col, fs_cor, fr_cor,
    pb, pr_row, ps_col, pr_col, ps_cor, pr_cor,
    xin, xup, xa, xb, wt, ut, gb, r0, h1, r1, h2, r2, h3, r3, tab,
    f_send, f_recv, p_send, p_recv, s0, s1s, s1r, s2s, s2r, s3, ts, tr,
):
    batch, height, breadth, ch = in_ref.shape
    halo = 2 * ITERS
    wide = breadth + 2 * halo
    cell_count, grad_scale = counts
    n = nr * nc
    half = nc // 2
    ri, ci, rp = lax.axis_index("rows"), lax.axis_index("cols"), lax.axis_index("rep")
    me = ri * nc + ci
    core, cy = lax.rem(ci, 2), ci // 2

    def dev(row, col, rep):
        return {"rows": row, "cols": col, "rep": rep}

    barrier = pltpu.get_barrier_semaphore()

    def greet(k, c):
        t = lax.rem(me + k, n)
        pl.semaphore_signal(
            barrier, inc=1, device_id=dev(t // nc, lax.rem(t, nc), rp), device_id_type=MESH
        )
        return c

    lax.fori_loop(1, n, greet, 0)
    pl.semaphore_signal(barrier, inc=1, device_id=dev(ri, ci, 1 - rp), device_id_type=MESH)

    for f, ref in ((0, in_ref), (1, up_ref)):
        lo = f * batch
        for s, row in ((0, 0), (1, height - 1)):
            fs_row[s, lo : lo + batch] = ref[:, row]
        for b in range(batch):
            x = ref[b].astype(F32)
            left, right = x[:, 0, :], x[:, breadth - 1, :]
            fs_col[0, lo + b] = left.astype(BF16)
            fs_col[1, lo + b] = right.astype(BF16)
            for h, edge in ((0, left), (1, right)):
                fs_cor[0, h, lo + b] = jnp.broadcast_to(edge[0:1], (16, ch)).astype(BF16)
                fs_cor[1, h, lo + b] = jnp.broadcast_to(
                    edge[height - 1 : height], (16, ch)
                ).astype(BF16)
    pb[...] = p_ref[...].astype(BF16)
    for h, col in ((0, 0), (1, breadth - halo)):
        edge = p_ref[:, col : col + halo, :]
        ps_col[h] = edge.reshape(height * halo // 16, 16, ch).astype(BF16)
        for v, row in ((0, 0), (1, height - halo)):
            ps_cor[v, h] = (
                edge[row : row + halo].reshape(halo * halo // 16, 16, ch).astype(BF16)
            )

    pl.semaphore_wait(barrier, n)

    def sidx(v):
        return 0 if v < 0 else 1

    def exists(v, h):
        ok = None
        for d, pos, size in ((v, ri, nr), (h, ci, nc)):
            if d:
                here = (pos > 0) if d < 0 else (pos < size - 1)
                ok = here if ok is None else jnp.logical_and(ok, here)
        return ok

    def target(v, h):
        return dev(lax.rem(ri + v + nr, nr), lax.rem(ci + h + nc, nc), rp)

    def buffers(v, h, row, col, cor):
        if h == 0:
            return row.at[sidx(v)]
        if v == 0:
            return col.at[sidx(h)]
        return cor.at[sidx(v), sidx(h)]

    def f_copy(k):
        v, h = SIDES[k]
        return pltpu.make_async_remote_copy(
            src_ref=buffers(v, h, fs_row, fs_col, fs_cor),
            dst_ref=buffers(-v, -h, fr_row, fr_col, fr_cor),
            send_sem=f_send.at[k],
            recv_sem=f_recv.at[k],
            device_id=target(v, h),
            device_id_type=MESH,
        )

    def p_copy(k):
        v, h = SIDES[k]
        if h == 0:
            src = pb.at[pl.ds(0 if v < 0 else height - halo, halo)]
        else:
            src = buffers(v, h, None, ps_col, ps_cor)
        return pltpu.make_async_remote_copy(
            src_ref=src,
            dst_ref=buffers(-v, -h, pr_row, pr_col, pr_cor),
            send_sem=p_send.at[k],
            recv_sem=p_recv.at[k],
            device_id=target(v, h),
            device_id_type=MESH,
        )

    for k, (v, h) in enumerate(SIDES):
        @pl.when(exists(v, h))
        def _(k=k):
            f_copy(k).start()

        @pl.when(jnp.logical_not(exists(v, h)))
        def _(v=v, h=h):
            ref = buffers(v, h, fr_row, fr_col, fr_cor)
            ref[...] = jnp.zeros(ref.shape, BF16)

    for k in range(8):
        p_copy(k).start()

    for a in range(3):
        for b in range(3):
            wt[a, b * ch : (b + 1) * ch, :] = k_ref[2 - a, 2 - b].T
    cells = height * breadth

    def turn(b, c):
        ut[b] = up_ref[b].reshape(cells, ch).T
        return c

    lax.fori_loop(0, batch, turn, 0)

    for k, (v, h) in enumerate(SIDES):
        @pl.when(exists(-v, -h))
        def _(k=k):
            f_copy(k).wait_recv()

    def put_padded(dst, b, row, value, lefts, rights):
        rows = value.shape[0]
        flat = value.reshape(rows * breadth, ch)
        j = lax.broadcasted_iota(jnp.int32, (rows, breadth, ch), 1)
        left = pltpu.roll(flat, 1, 0).reshape(rows, breadth, ch)
        right = pltpu.roll(flat, rows * breadth - 1, 0).reshape(rows, breadth, ch)
        left = jnp.where(j == 0, lefts[:, None, :], left)
        right = jnp.where(j == breadth - 1, rights[:, None, :], right)
        dst[b, row : row + rows, :, 0:ch] = left.astype(BF16)
        dst[b, row : row + rows, :, ch : 2 * ch] = value.astype(BF16)
        dst[b, row : row + rows, :, 2 * ch :] = right.astype(BF16)

    def pad_fields(f, ref, dst):
        def step(b, c):
            e = f * batch + b
            put_padded(
                dst, b, 1, ref[b].astype(F32),
                fr_col[0, e].astype(F32), fr_col[1, e].astype(F32),
            )
            for s, row in ((0, 0), (1, height + 1)):
                put_padded(
                    dst, b, row, fr_row[s, e].astype(F32)[None],
                    fr_cor[s, 0, e].astype(F32)[0:1], fr_cor[s, 1, e].astype(F32)[0:1],
                )
            return c

        lax.fori_loop(0, batch, step, 0)

    pad_fields(0, in_ref, xin)

    dper = ch // n

    def grad_step(a, c):
        for b in range(3):
            acc = None
            for m in range(batch):
                window = xin[m, pl.ds(a, height), :, b * ch : (b + 1) * ch]
                term = jnp.dot(
                    ut[m], window.reshape(cells, ch), preferred_element_type=F32
                )
                acc = term if acc is None else acc + term
            at = pl.multiple_of(a * (3 * ch) + b * ch, 128)
            for t in range(n):
                rr, cc = t // nc, t % nc
                gb[cc % 2, cc // 2, rr, :, pl.ds(at, ch)] = acc[
                    t * dper : (t + 1) * dper
                ].astype(BF16)
        return c

    lax.fori_loop(0, 3, grad_step, 0)

    def copy0():
        return pltpu.make_async_remote_copy(
            src_ref=gb.at[1 - core],
            dst_ref=r0,
            send_sem=s0.at[0],
            recv_sem=s0.at[1],
            device_id=dev(ri, ci + 1 - 2 * core, rp),
            device_id_type=MESH,
        )

    def copy1(k):
        to = lax.rem(cy + k, half)
        return pltpu.make_async_remote_copy(
            src_ref=h1.at[to],
            dst_ref=r1.at[k - 1],
            send_sem=s1s.at[k - 1],
            recv_sem=s1r.at[k - 1],
            device_id=dev(ri, to * 2 + core, rp),
            device_id_type=MESH,
        )

    def copy2(k):
        to = lax.rem(ri + k, nr)
        return pltpu.make_async_remote_copy(
            src_ref=h2.at[to],
            dst_ref=r2.at[k - 1],
            send_sem=s2s.at[k - 1],
            recv_sem=s2r.at[k - 1],
            device_id=dev(to, ci, rp),
            device_id_type=MESH,
        )

    def copy3():
        return pltpu.make_async_remote_copy(
            src_ref=h3,
            dst_ref=r3,
            send_sem=s3.at[0],
            recv_sem=s3.at[1],
            device_id=dev(ri, ci, 1 - rp),
            device_id_type=MESH,
        )

    copy0().start()

    def field_conv(src, dst, weights):
        block = min(height, 8)

        def step(t, c):
            b, row = t // (height // block), lax.rem(t, height // block) * block
            acc = None
            for a in range(3):
                window = src[b, pl.ds(row + a, block)].reshape(block * breadth, 3 * ch)
                term = jnp.dot(window, weights(a), preferred_element_type=F32)
                acc = term if acc is None else acc + term
            dst[b, pl.ds(row, block)] = acc.reshape(block, breadth, ch).astype(BF16)
            return c

        lax.fori_loop(0, batch * (height // block), step, 0)

    def forward(a):
        return k_ref[a].reshape(3 * ch, ch)

    def adjoint(a):
        return wt[a]

    field_conv(xin, o_ref, forward)

    copy0().wait_recv()

    def sum0(t, c):
        a, b = t // nr, lax.rem(t, nr)
        h1[a, b] = (gb[core, a, b].astype(F32) + r0[a, b].astype(F32)).astype(BF16)
        return c

    lax.fori_loop(0, half * nr, sum0, 0)
    for k in range(1, half):
        copy1(k).start()

    pad_fields(1, up_ref, xup)

    def put(dst, row, value):
        rows = value.shape[0]
        flat = value.reshape(rows * wide, ch)
        left = pltpu.roll(flat, 1, 0)
        right = pltpu.roll(flat, rows * wide - 1, 0)
        dst[pl.ds(row, rows), :, 0:ch] = left.reshape(rows, wide, ch).astype(BF16)
        dst[pl.ds(row, rows), :, ch : 2 * ch] = value.astype(BF16)
        dst[pl.ds(row, rows), :, 2 * ch :] = right.reshape(rows, wide, ch).astype(BF16)

    for k in range(8):
        p_copy(k).wait_recv()
    for s, row in ((0, 0), (1, height + halo)):
        put(
            xa, row,
            jnp.concatenate(
                [
                    pr_cor[s, 0].astype(F32).reshape(halo, halo, ch),
                    pr_row[s].astype(F32),
                    pr_cor[s, 1].astype(F32).reshape(halo, halo, ch),
                ],
                axis=1,
            ),
        )
    put(
        xa, halo,
        jnp.concatenate(
            [
                pr_col[0].astype(F32).reshape(height, halo, ch),
                pb[...].astype(F32),
                pr_col[1].astype(F32).reshape(height, halo, ch),
            ],
            axis=1,
        ),
    )

    def tile_conv(src, row, block, weights):
        acc = None
        for a in range(3):
            window = src[pl.ds(row + a, block)].reshape(block * wide, 3 * ch)
            term = jnp.dot(window, weights(a), preferred_element_type=F32)
            acc = term if acc is None else acc + term
        return acc

    def fold(x):
        return jnp.sum(x.reshape(-1, 8, ch), axis=0)

    def total(x):
        return jnp.sum(jnp.sum(x, axis=0, keepdims=True), axis=1, keepdims=True)

    def note(row, value):
        tab[me, row : row + 1, :] = jnp.broadcast_to(value, (1, 128))

    factor = None
    rows = height + 2 * halo
    for it in range(ITERS):
        rows -= 2
        block = split_rows(rows)

        def ahead(t, c, block=block, factor=factor):
            acc = tile_conv(xa, t * block, block, forward)
            if factor is not None:
                acc = acc * factor
            put(xb, t * block, acc.reshape(block, wide, ch))
            return c

        lax.fori_loop(0, rows // block, ahead, 0)
        rows -= 2
        block = split_rows(rows)
        first = (rows - height) // 2
        last = it + 1 == ITERS

        def back(t, c, block=block, first=first, last=last):
            own, every, rounded = c
            acc = tile_conv(xb, t * block, block, adjoint)
            full = acc.reshape(block, wide, ch)
            mine = full[:, halo : halo + breadth, :]
            if last:
                po_ref[pl.ds(t * block, block)] = mine
                return own + fold(mine * mine), every, rounded
            put(xa, t * block, full)
            where = t * block + lax.broadcasted_iota(jnp.int32, mine.shape, 0)
            inside = jnp.logical_and(where >= first, where < first + height)
            mine = jnp.where(inside, mine, 0.0)
            near = mine.astype(BF16).astype(F32)
            return (
                own + fold(mine * mine),
                every + fold(acc * acc),
                rounded + fold(near * near),
            )

        zero = jnp.zeros((8, ch), F32)
        own, every, rounded = lax.fori_loop(0, rows // block, back, (zero, zero, zero))
        note(it, total(own))
        if it == ITERS - 2:
            note(ITERS, total(rounded))
        if not last:
            mean = total(every) / float(rows * wide * ch)
            root = jnp.sqrt(jnp.maximum(mean, 1e-30))
            factor = 1.0 / root
            note(ITERS + 1 + it, root)
        if it == 0:
            for k in range(1, half):
                copy1(k).wait_recv()

            def sum1(b, c):
                acc = h1[cy, b].astype(F32)
                for k in range(1, half):
                    acc = acc + r1[k - 1, b].astype(F32)
                h2[b] = acc.astype(BF16)
                return c

            lax.fori_loop(0, nr, sum1, 0)
            for k in range(1, nr):
                copy2(k).start()
        if it == ITERS - 2:
            for k in range(1, nr):
                copy2(k).wait_recv()
            acc = h2[ri].astype(F32)
            for k in range(1, nr):
                acc = acc + r2[k - 1].astype(F32)
            h3[...] = acc
            copy3().start()

    def copyt(k):
        to = lax.rem(me + k, n)
        return pltpu.make_async_remote_copy(
            src_ref=tab.at[me],
            dst_ref=tab.at[me],
            send_sem=ts.at[k],
            recv_sem=tr.at[k],
            device_id=dev(to // nc, lax.rem(to, nc), rp),
            device_id_type=MESH,
        )

    def copyt_in(k):
        of = lax.rem(me - k + n, n)
        return pltpu.make_async_remote_copy(
            src_ref=tab.at[me],
            dst_ref=tab.at[of],
            send_sem=ts.at[k],
            recv_sem=tr.at[k],
            device_id=dev(of // nc, lax.rem(of, nc), rp),
            device_id_type=MESH,
        )

    def tell(k, c):
        copyt(k).start()
        return c

    lax.fori_loop(1, n, tell, 0)

    field_conv(xup, g_ref, adjoint)

    def hear(k, c):
        copyt_in(k).wait_recv()
        return c

    lax.fori_loop(1, n, hear, 0)
    told = tab[...]
    gain = jnp.ones((n, 128), F32)
    for it in range(ITERS - 1):
        squared = jnp.sum(told[:, it, :] * gain * gain, axis=0, keepdims=True)
        scale = jnp.sqrt(squared / cell_count + 1e-06)
        sc_ref[it + 1 : it + 2, :] = scale
        gain = gain / scale
        if it == ITERS - 2:
            sum_probe = jnp.sum(told[:, ITERS, :] * gain * gain, axis=0, keepdims=True)
        gain = gain * told[:, ITERS + 1 + it, :]
    sum_back = jnp.sum(told[:, ITERS - 1, :] * gain * gain, axis=0, keepdims=True)
    sc_ref[0:1, :] = jnp.sqrt(jnp.sqrt(sum_back / sum_probe))
    own_gain = 1.0 / jnp.sqrt(sum_back / cell_count + 1e-06)
    for it in range(ITERS - 1):
        own_gain = own_gain * tab[me, ITERS + 1 + it : ITERS + 2 + it, :]
        own_gain = own_gain / sc_ref[it + 1 : it + 2, :]
    both = jnp.concatenate([own_gain] * (ch // 128), axis=1).reshape(1, 1, ch)
    po_ref[...] = po_ref[...] * both

    copy3().wait_recv()
    kg_ref[...] = (h3[...] + r3[...]) * grad_scale

    for k, (v, h) in enumerate(SIDES):
        @pl.when(exists(v, h))
        def _(k=k):
            f_copy(k).wait_send()

        p_copy(k).wait_send()
    copy0().wait_send()
    for k in range(1, half):
        copy1(k).wait_send()
    for k in range(1, nr):
        copy2(k).wait_send()
    copy3().wait_send()

    def sent(k, c):
        copyt(k).wait_send()
        return c

    lax.fori_loop(1, n, sent, 0)


def solution(mesh):
    nr, nc = mesh.shape["rows"], mesh.shape["cols"]
    reps = mesh.shape["rep"]

    def per_device(inputs, upstream, weights, probe_init):
        batch, height, breadth, ch = inputs.shape
        n = nr * nc
        half = nc // 2
        dper = ch // n
        halo = 2 * ITERS
        wide = breadth + 2 * halo
        cell_count = float(height * nr * breadth * nc * ch)
        grad_scale = 1.0 / math.sqrt(batch * reps * height * nr * breadth * nc)
        cells = height * breadth
        sem = pltpu.SemaphoreType.DMA
        vmem = pl.BlockSpec(memory_space=pltpu.VMEM)
        scratch = [
            ((2, 2 * batch, breadth, ch), BF16),
            ((2, 2 * batch, breadth, ch), BF16),
            ((2, 2 * batch, height, ch), BF16),
            ((2, 2 * batch, height, ch), BF16),
            ((2, 2, 2 * batch, 16, ch), BF16),
            ((2, 2, 2 * batch, 16, ch), BF16),
            ((height, breadth, ch), BF16),
            ((2, halo, breadth, ch), BF16),
            ((2, height * halo // 16, 16, ch), BF16),
            ((2, height * halo // 16, 16, ch), BF16),
            ((2, 2, halo * halo // 16, 16, ch), BF16),
            ((2, 2, halo * halo // 16, 16, ch), BF16),
            ((batch, height + 2, breadth, 3 * ch), BF16),
            ((batch, height + 2, breadth, 3 * ch), BF16),
            ((height + 2 * halo, wide, 3 * ch), BF16),
            ((height + 2 * halo, wide, 3 * ch), BF16),
            ((3, 3 * ch, ch), BF16),
            ((batch, ch, cells), BF16),
            ((2, half, nr, dper, 9 * ch), BF16),
            ((half, nr, dper, 9 * ch), BF16),
            ((half, nr, dper, 9 * ch), BF16),
            ((half - 1, nr, dper, 9 * ch), BF16),
            ((nr, dper, 9 * ch), BF16),
            ((nr - 1, dper, 9 * ch), BF16),
            ((dper, 9 * ch), F32),
            ((dper, 9 * ch), F32),
            ((n, 8, 128), F32),
        ]
        outs = pl.pallas_call(
            functools.partial(kernel, nr, nc, (cell_count, grad_scale)),
            out_shape=(
                jax.ShapeDtypeStruct(inputs.shape, BF16),
                jax.ShapeDtypeStruct(inputs.shape, BF16),
                jax.ShapeDtypeStruct((dper, 9 * ch), F32),
                jax.ShapeDtypeStruct(probe_init.shape, F32),
                jax.ShapeDtypeStruct((8, 128), F32),
            ),
            in_specs=[vmem] * 4,
            out_specs=[vmem] * 5,
            scratch_shapes=[pltpu.VMEM(s, t) for s, t in scratch]
            + [
                sem((8,)), sem((8,)), sem((8,)), sem((8,)), sem((2,)),
                sem((max(half - 1, 1),)), sem((max(half - 1, 1),)),
                sem((nr - 1,)), sem((nr - 1,)), sem((2,)), sem((n,)), sem((n,)),
            ],
            compiler_params=pltpu.CompilerParams(
                collective_id=0, has_side_effects=True, vmem_limit_bytes=60 * 2**20
            ),
        )(inputs, upstream, weights, probe_init)
        outputs, input_grad, kernel_grad, probe_out, scalars = outs
        return (
            outputs, input_grad, kernel_grad, probe_out,
            scalars[0, 0], scalars[1:ITERS, 0],
        )

    placed = (
        P("rep", "rows", "cols", None),
        P("rep", "rows", "cols", None),
        P(),
        P("rows", "cols", None),
    )
    return jax.shard_map(
        per_device,
        mesh=mesh,
        in_specs=placed,
        out_specs=(
            P("rep", "rows", "cols", None),
            P("rep", "rows", "cols", None),
            P(("rows", "cols"), None),
            P("rows", "cols", None),
            P(),
            P(),
        ),
        check_vma=False,
    )
```

```python
import functools
import math

import jax
import jax.numpy as jnp
from jax import lax
from jax.experimental import pallas as pl
from jax.experimental.pallas import tpu as pltpu
from jax.sharding import PartitionSpec as P

MESH = pl.DeviceIdType.MESH
ITERS = 4
F32 = jnp.float32
BF16 = jnp.bfloat16
SIDES = [(v, h) for v in (-1, 0, 1) for h in (-1, 0, 1) if (v, h) != (0, 0)]


def split_rows(rows):
    for block in (13, 11, 10, 9, 8, 7, 6, 5, 4, 3, 2):
        if rows % block == 0:
            return block
    return 1


def kernel(
    nr, nc, counts, in_hbm, up_hbm, k_hbm, p_hbm,
    o_hbm, g_hbm, kg_ref, po_ref, sc_ref,
    in_ref, up_ref, k_ref, p_ref, o_ref, g_ref, load, store,
    fs_row, fr_row, fs_col, fr_col, fs_cor, fr_cor,
    pb, pr_row, ps_col, pr_col, ps_cor, pr_cor,
    xin, xup, xa, xb, wt, ut, gb, r0, h1, r1, h2, r2, h3, r3, tab,
    f_send, f_recv, p_send, p_recv, s0, s1s, s1r, s2s, s2r, s3, ts, tr,
):
    batch, height, breadth, ch = in_ref.shape
    halo = 2 * ITERS
    wide = breadth + 2 * halo
    cell_count, grad_scale = counts
    loads = [
        pltpu.make_async_copy(src, dst, load.at[i])
        for i, (src, dst) in enumerate(
            ((in_hbm, in_ref), (up_hbm, up_ref), (p_hbm, p_ref), (k_hbm, k_ref))
        )
    ]
    stores = [
        pltpu.make_async_copy(src, dst, store.at[i])
        for i, (src, dst) in enumerate(((o_ref, o_hbm), (g_ref, g_hbm)))
    ]
    for one in loads:
        one.start()
    n = nr * nc
    half = nc // 2
    ri, ci, rp = lax.axis_index("rows"), lax.axis_index("cols"), lax.axis_index("rep")
    me = ri * nc + ci
    core, cy = lax.rem(ci, 2), ci // 2

    def dev(row, col, rep):
        return {"rows": row, "cols": col, "rep": rep}

    barrier = pltpu.get_barrier_semaphore()

    def greet(k, c):
        t = lax.rem(me + k, n)
        pl.semaphore_signal(
            barrier, inc=1, device_id=dev(t // nc, lax.rem(t, nc), rp), device_id_type=MESH
        )
        return c

    lax.fori_loop(1, n, greet, 0)
    pl.semaphore_signal(barrier, inc=1, device_id=dev(ri, ci, 1 - rp), device_id_type=MESH)

    for f, ref in ((0, in_ref), (1, up_ref)):
        lo = f * batch
        loads[f].wait()
        for s, row in ((0, 0), (1, height - 1)):
            fs_row[s, lo : lo + batch] = ref[:, row]
        for b in range(batch):
            x = ref[b].astype(F32)
            left, right = x[:, 0, :], x[:, breadth - 1, :]
            fs_col[0, lo + b] = left.astype(BF16)
            fs_col[1, lo + b] = right.astype(BF16)
            for h, edge in ((0, left), (1, right)):
                fs_cor[0, h, lo + b] = jnp.broadcast_to(edge[0:1], (16, ch)).astype(BF16)
                fs_cor[1, h, lo + b] = jnp.broadcast_to(
                    edge[height - 1 : height], (16, ch)
                ).astype(BF16)
    loads[2].wait()
    pb[...] = p_ref[...].astype(BF16)
    for h, col in ((0, 0), (1, breadth - halo)):
        edge = p_ref[:, col : col + halo, :]
        ps_col[h] = edge.reshape(height * halo // 16, 16, ch).astype(BF16)
        for v, row in ((0, 0), (1, height - halo)):
            ps_cor[v, h] = (
                edge[row : row + halo].reshape(halo * halo // 16, 16, ch).astype(BF16)
            )

    pl.semaphore_wait(barrier, n)

    def sidx(v):
        return 0 if v < 0 else 1

    def exists(v, h):
        ok = None
        for d, pos, size in ((v, ri, nr), (h, ci, nc)):
            if d:
                here = (pos > 0) if d < 0 else (pos < size - 1)
                ok = here if ok is None else jnp.logical_and(ok, here)
        return ok

    def target(v, h):
        return dev(lax.rem(ri + v + nr, nr), lax.rem(ci + h + nc, nc), rp)

    def buffers(v, h, row, col, cor):
        if h == 0:
            return row.at[sidx(v)]
        if v == 0:
            return col.at[sidx(h)]
        return cor.at[sidx(v), sidx(h)]

    def f_copy(k):
        v, h = SIDES[k]
        return pltpu.make_async_remote_copy(
            src_ref=buffers(v, h, fs_row, fs_col, fs_cor),
            dst_ref=buffers(-v, -h, fr_row, fr_col, fr_cor),
            send_sem=f_send.at[k],
            recv_sem=f_recv.at[k],
            device_id=target(v, h),
            device_id_type=MESH,
        )

    def p_copy(k):
        v, h = SIDES[k]
        if h == 0:
            src = pb.at[pl.ds(0 if v < 0 else height - halo, halo)]
        else:
            src = buffers(v, h, None, ps_col, ps_cor)
        return pltpu.make_async_remote_copy(
            src_ref=src,
            dst_ref=buffers(-v, -h, pr_row, pr_col, pr_cor),
            send_sem=p_send.at[k],
            recv_sem=p_recv.at[k],
            device_id=target(v, h),
            device_id_type=MESH,
        )

    for k, (v, h) in enumerate(SIDES):
        @pl.when(exists(v, h))
        def _(k=k):
            f_copy(k).start()

        @pl.when(jnp.logical_not(exists(v, h)))
        def _(v=v, h=h):
            ref = buffers(v, h, fr_row, fr_col, fr_cor)
            ref[...] = jnp.zeros(ref.shape, BF16)

    for k in range(8):
        p_copy(k).start()

    loads[3].wait()

    for a in range(3):
        for b in range(3):
            wt[a, b * ch : (b + 1) * ch, :] = k_ref[2 - a, 2 - b].T
    cells = height * breadth

    def turn(b, c):
        ut[:, pl.ds(pl.multiple_of(b * cells, 128), cells)] = (
            up_ref[b].reshape(cells, ch).T
        )
        return c

    lax.fori_loop(0, batch, turn, 0)

    for k, (v, h) in enumerate(SIDES):
        @pl.when(exists(-v, -h))
        def _(k=k):
            f_copy(k).wait_recv()

    def put_padded(dst, b, row, value, lefts, rights):
        rows = value.shape[0]
        flat = value.reshape(rows * breadth, ch)
        j = lax.broadcasted_iota(jnp.int32, (rows, breadth, ch), 1)
        left = pltpu.roll(flat, 1, 0).reshape(rows, breadth, ch)
        right = pltpu.roll(flat, rows * breadth - 1, 0).reshape(rows, breadth, ch)
        left = jnp.where(j == 0, lefts[:, None, :], left)
        right = jnp.where(j == breadth - 1, rights[:, None, :], right)
        dst[b, row : row + rows, :, 0:ch] = left.astype(BF16)
        dst[b, row : row + rows, :, ch : 2 * ch] = value.astype(BF16)
        dst[b, row : row + rows, :, 2 * ch :] = right.astype(BF16)

    def pad_fields(f, ref, dst):
        def step(b, c):
            e = f * batch + b
            put_padded(
                dst, b, 1, ref[b].astype(F32),
                fr_col[0, e].astype(F32), fr_col[1, e].astype(F32),
            )
            for s, row in ((0, 0), (1, height + 1)):
                put_padded(
                    dst, b, row, fr_row[s, e].astype(F32)[None],
                    fr_cor[s, 0, e].astype(F32)[0:1], fr_cor[s, 1, e].astype(F32)[0:1],
                )
            return c

        lax.fori_loop(0, batch, step, 0)

    pad_fields(0, in_ref, xin)

    dper = ch // n

    def grad_step(a, c):
        for b in range(3):
            window = xin[:, pl.ds(a, height), :, b * ch : (b + 1) * ch]
            acc = jnp.dot(
                ut[...], window.reshape(batch * cells, ch), preferred_element_type=F32
            )
            at = pl.multiple_of(a * (3 * ch) + b * ch, 128)
            for t in range(n):
                rr, cc = t // nc, t % nc
                gb[cc % 2, cc // 2, rr, :, pl.ds(at, ch)] = acc[
                    t * dper : (t + 1) * dper
                ].astype(BF16)
        return c

    lax.fori_loop(0, 3, grad_step, 0)

    def copy0():
        return pltpu.make_async_remote_copy(
            src_ref=gb.at[1 - core],
            dst_ref=r0,
            send_sem=s0.at[0],
            recv_sem=s0.at[1],
            device_id=dev(ri, ci + 1 - 2 * core, rp),
            device_id_type=MESH,
        )

    def copy1(k):
        to = lax.rem(cy + k, half)
        return pltpu.make_async_remote_copy(
            src_ref=h1.at[to],
            dst_ref=r1.at[k - 1],
            send_sem=s1s.at[k - 1],
            recv_sem=s1r.at[k - 1],
            device_id=dev(ri, to * 2 + core, rp),
            device_id_type=MESH,
        )

    def copy2(k):
        to = lax.rem(ri + k, nr)
        return pltpu.make_async_remote_copy(
            src_ref=h2.at[to],
            dst_ref=r2.at[k - 1],
            send_sem=s2s.at[k - 1],
            recv_sem=s2r.at[k - 1],
            device_id=dev(to, ci, rp),
            device_id_type=MESH,
        )

    def copy3():
        return pltpu.make_async_remote_copy(
            src_ref=h3,
            dst_ref=r3,
            send_sem=s3.at[0],
            recv_sem=s3.at[1],
            device_id=dev(ri, ci, 1 - rp),
            device_id_type=MESH,
        )

    copy0().start()

    def field_conv(src, dst, weights):
        block = min(height, 8)

        def step(t, c):
            b, row = t // (height // block), lax.rem(t, height // block) * block
            windows = [
                src[b, pl.ds(row + a, block)].reshape(block * breadth, 3 * ch)
                for a in range(3)
            ]
            acc = jnp.dot(
                jnp.concatenate(windows, axis=1), weights(), preferred_element_type=F32
            )
            dst[b, pl.ds(row, block)] = acc.reshape(block, breadth, ch).astype(BF16)
            return c

        lax.fori_loop(0, batch * (height // block), step, 0)

    def forward():
        return k_ref[...].reshape(9 * ch, ch)

    def adjoint():
        return wt[...].reshape(9 * ch, ch)

    field_conv(xin, o_ref, forward)
    stores[0].start()

    copy0().wait_recv()

    def sum0(t, c):
        a, b = t // nr, lax.rem(t, nr)
        h1[a, b] = (gb[core, a, b].astype(F32) + r0[a, b].astype(F32)).astype(BF16)
        return c

    lax.fori_loop(0, half * nr, sum0, 0)
    for k in range(1, half):
        copy1(k).start()

    pad_fields(1, up_ref, xup)

    def put(dst, row, value):
        rows = value.shape[0]
        flat = value.reshape(rows * wide, ch)
        left = pltpu.roll(flat, 1, 0)
        right = pltpu.roll(flat, rows * wide - 1, 0)
        dst[pl.ds(row, rows), :, 0:ch] = left.reshape(rows, wide, ch).astype(BF16)
        dst[pl.ds(row, rows), :, ch : 2 * ch] = value.astype(BF16)
        dst[pl.ds(row, rows), :, 2 * ch :] = right.reshape(rows, wide, ch).astype(BF16)

    for k in range(8):
        p_copy(k).wait_recv()
    for s, row in ((0, 0), (1, height + halo)):
        put(
            xa, row,
            jnp.concatenate(
                [
                    pr_cor[s, 0].astype(F32).reshape(halo, halo, ch),
                    pr_row[s].astype(F32),
                    pr_cor[s, 1].astype(F32).reshape(halo, halo, ch),
                ],
                axis=1,
            ),
        )
    put(
        xa, halo,
        jnp.concatenate(
            [
                pr_col[0].astype(F32).reshape(height, halo, ch),
                pb[...].astype(F32),
                pr_col[1].astype(F32).reshape(height, halo, ch),
            ],
            axis=1,
        ),
    )

    def tile_conv(src, row, block, weights):
        windows = [
            src[pl.ds(row + a, block)].reshape(block * wide, 3 * ch) for a in range(3)
        ]
        return jnp.dot(
            jnp.concatenate(windows, axis=1), weights(), preferred_element_type=F32
        )

    def fold(x):
        return jnp.sum(x.reshape(-1, 8, ch), axis=0)

    def total(x):
        return jnp.sum(jnp.sum(x, axis=0, keepdims=True), axis=1, keepdims=True)

    def note(row, value):
        tab[me, row : row + 1, :] = jnp.broadcast_to(value, (1, 128))

    factor = None
    rows = height + 2 * halo
    for it in range(ITERS):
        rows -= 2
        block = split_rows(rows)

        def ahead(t, c, block=block, factor=factor):
            acc = tile_conv(xa, t * block, block, forward)
            if factor is not None:
                acc = acc * factor
            put(xb, t * block, acc.reshape(block, wide, ch))
            return c

        lax.fori_loop(0, rows // block, ahead, 0)
        rows -= 2
        block = split_rows(rows)
        first = (rows - height) // 2
        last = it + 1 == ITERS

        def back(t, c, block=block, first=first, last=last):
            own, every, rounded = c
            acc = tile_conv(xb, t * block, block, adjoint)
            full = acc.reshape(block, wide, ch)
            mine = full[:, halo : halo + breadth, :]
            if last:
                po_ref[pl.ds(t * block, block)] = mine
                return own + fold(mine * mine), every, rounded
            put(xa, t * block, full)
            where = t * block + lax.broadcasted_iota(jnp.int32, mine.shape, 0)
            inside = jnp.logical_and(where >= first, where < first + height)
            mine = jnp.where(inside, mine, 0.0)
            near = mine.astype(BF16).astype(F32)
            return (
                own + fold(mine * mine),
                every + fold(acc * acc),
                rounded + fold(near * near),
            )

        zero = jnp.zeros((8, ch), F32)
        own, every, rounded = lax.fori_loop(0, rows // block, back, (zero, zero, zero))
        note(it, total(own))
        if it == ITERS - 2:
            note(ITERS, total(rounded))
        if not last:
            mean = total(every) / float(rows * wide * ch)
            root = jnp.sqrt(jnp.maximum(mean, 1e-30))
            factor = 1.0 / root
            note(ITERS + 1 + it, root)
        if it == 0:
            for k in range(1, half):
                copy1(k).wait_recv()

            def sum1(b, c):
                acc = h1[cy, b].astype(F32)
                for k in range(1, half):
                    acc = acc + r1[k - 1, b].astype(F32)
                h2[b] = acc.astype(BF16)
                return c

            lax.fori_loop(0, nr, sum1, 0)
            for k in range(1, nr):
                copy2(k).start()
        if it == ITERS - 2:
            for k in range(1, nr):
                copy2(k).wait_recv()
            acc = h2[ri].astype(F32)
            for k in range(1, nr):
                acc = acc + r2[k - 1].astype(F32)
            h3[...] = acc
            copy3().start()

    def copyt(k):
        to = lax.rem(me + k, n)
        return pltpu.make_async_remote_copy(
            src_ref=tab.at[me],
            dst_ref=tab.at[me],
            send_sem=ts.at[k],
            recv_sem=tr.at[k],
            device_id=dev(to // nc, lax.rem(to, nc), rp),
            device_id_type=MESH,
        )

    def copyt_in(k):
        of = lax.rem(me - k + n, n)
        return pltpu.make_async_remote_copy(
            src_ref=tab.at[me],
            dst_ref=tab.at[of],
            send_sem=ts.at[k],
            recv_sem=tr.at[k],
            device_id=dev(of // nc, lax.rem(of, nc), rp),
            device_id_type=MESH,
        )

    def tell(k, c):
        copyt(k).start()
        return c

    lax.fori_loop(1, n, tell, 0)

    field_conv(xup, g_ref, adjoint)
    stores[1].start()

    def hear(k, c):
        copyt_in(k).wait_recv()
        return c

    lax.fori_loop(1, n, hear, 0)
    told = tab[...]
    gain = jnp.ones((n, 128), F32)
    for it in range(ITERS - 1):
        squared = jnp.sum(told[:, it, :] * gain * gain, axis=0, keepdims=True)
        scale = jnp.sqrt(squared / cell_count + 1e-06)
        sc_ref[it + 1 : it + 2, :] = scale
        gain = gain / scale
        if it == ITERS - 2:
            sum_probe = jnp.sum(told[:, ITERS, :] * gain * gain, axis=0, keepdims=True)
        gain = gain * told[:, ITERS + 1 + it, :]
    sum_back = jnp.sum(told[:, ITERS - 1, :] * gain * gain, axis=0, keepdims=True)
    sc_ref[0:1, :] = jnp.sqrt(jnp.sqrt(sum_back / sum_probe))
    own_gain = 1.0 / jnp.sqrt(sum_back / cell_count + 1e-06)
    for it in range(ITERS - 1):
        own_gain = own_gain * tab[me, ITERS + 1 + it : ITERS + 2 + it, :]
        own_gain = own_gain / sc_ref[it + 1 : it + 2, :]
    both = jnp.concatenate([own_gain] * (ch // 128), axis=1).reshape(1, 1, ch)
    po_ref[...] = po_ref[...] * both

    copy3().wait_recv()
    kg_ref[...] = (h3[...] + r3[...]) * grad_scale

    for k, (v, h) in enumerate(SIDES):
        @pl.when(exists(v, h))
        def _(k=k):
            f_copy(k).wait_send()

        p_copy(k).wait_send()
    copy0().wait_send()
    for k in range(1, half):
        copy1(k).wait_send()
    for k in range(1, nr):
        copy2(k).wait_send()
    copy3().wait_send()

    for one in stores:
        one.wait()

    def sent(k, c):
        copyt(k).wait_send()
        return c

    lax.fori_loop(1, n, sent, 0)


def finish(o_in, g_in, kg_in, po_in, sc_in, o_out, g_out, kg_out, po_out, lip, trace, sems):
    copies = []
    for a in range(o_in.shape[0]):
        copies.append((o_in.at[a], o_out.at[a]))
        copies.append((g_in.at[a], g_out.at[a]))
    copies.append((po_in, po_out))
    copies.append((kg_in, kg_out))
    started = [
        pltpu.make_async_copy(src, dst, sems.at[i]) for i, (src, dst) in enumerate(copies)
    ]
    for one in started:
        one.start()
    lip[0] = sc_in[0, 0]
    for i in range(ITERS - 1):
        trace[i] = sc_in[i + 1, 0]
    for one in started:
        one.wait()


def solution(mesh):
    nr, nc = mesh.shape["rows"], mesh.shape["cols"]
    reps = mesh.shape["rep"]

    def per_device(inputs, upstream, weights, probe_init):
        batch, height, breadth, ch = inputs.shape
        n = nr * nc
        half = nc // 2
        dper = ch // n
        halo = 2 * ITERS
        wide = breadth + 2 * halo
        cell_count = float(height * nr * breadth * nc * ch)
        grad_scale = 1.0 / math.sqrt(batch * reps * height * nr * breadth * nc)
        cells = height * breadth
        sem = pltpu.SemaphoreType.DMA
        vmem = pl.BlockSpec(memory_space=pltpu.VMEM)
        scratch = [
            ((2, 2 * batch, breadth, ch), BF16),
            ((2, 2 * batch, breadth, ch), BF16),
            ((2, 2 * batch, height, ch), BF16),
            ((2, 2 * batch, height, ch), BF16),
            ((2, 2, 2 * batch, 16, ch), BF16),
            ((2, 2, 2 * batch, 16, ch), BF16),
            ((height, breadth, ch), BF16),
            ((2, halo, breadth, ch), BF16),
            ((2, height * halo // 16, 16, ch), BF16),
            ((2, height * halo // 16, 16, ch), BF16),
            ((2, 2, halo * halo // 16, 16, ch), BF16),
            ((2, 2, halo * halo // 16, 16, ch), BF16),
            ((batch, height + 2, breadth, 3 * ch), BF16),
            ((batch, height + 2, breadth, 3 * ch), BF16),
            ((height + 2 * halo, wide, 3 * ch), BF16),
            ((height + 2 * halo, wide, 3 * ch), BF16),
            ((3, 3 * ch, ch), BF16),
            ((ch, batch * cells), BF16),
            ((2, half, nr, dper, 9 * ch), BF16),
            ((half, nr, dper, 9 * ch), BF16),
            ((half, nr, dper, 9 * ch), BF16),
            ((half - 1, nr, dper, 9 * ch), BF16),
            ((nr, dper, 9 * ch), BF16),
            ((nr - 1, dper, 9 * ch), BF16),
            ((dper, 9 * ch), F32),
            ((dper, 9 * ch), F32),
            ((n, 8, 128), F32),
        ]
        anywhere = pl.BlockSpec(memory_space=pl.ANY)
        staged = [
            (inputs.shape, BF16), (inputs.shape, BF16), (weights.shape, BF16),
            (probe_init.shape, F32), (inputs.shape, BF16), (inputs.shape, BF16),
        ]
        outs = pl.pallas_call(
            functools.partial(kernel, nr, nc, (cell_count, grad_scale)),
            out_shape=(
                jax.ShapeDtypeStruct(inputs.shape, BF16),
                jax.ShapeDtypeStruct(inputs.shape, BF16),
                jax.ShapeDtypeStruct((dper, 9 * ch), F32),
                jax.ShapeDtypeStruct(probe_init.shape, F32),
                jax.ShapeDtypeStruct((8, 128), F32),
            ),
            in_specs=[anywhere] * 4,
            out_specs=[anywhere] * 2 + [vmem] * 3,
            scratch_shapes=[pltpu.VMEM(s, t) for s, t in staged]
            + [sem((4,)), sem((2,))]
            + [pltpu.VMEM(s, t) for s, t in scratch]
            + [
                sem((8,)), sem((8,)), sem((8,)), sem((8,)), sem((2,)),
                sem((max(half - 1, 1),)), sem((max(half - 1, 1),)),
                sem((nr - 1,)), sem((nr - 1,)), sem((2,)), sem((n,)), sem((n,)),
            ],
            compiler_params=pltpu.CompilerParams(
                collective_id=0, has_side_effects=True, vmem_limit_bytes=60 * 2**20
            ),
        )(inputs, upstream, weights, probe_init)
        smem = pl.BlockSpec(memory_space=pltpu.SMEM)
        *arrays, lipschitz, norm_trace = pl.pallas_call(
            finish,
            out_shape=tuple(jax.ShapeDtypeStruct(x.shape, x.dtype) for x in outs[:4])
            + (jax.ShapeDtypeStruct((1,), F32), jax.ShapeDtypeStruct((ITERS - 1,), F32)),
            in_specs=[anywhere] * 4 + [smem],
            out_specs=[anywhere] * 4 + [smem] * 2,
            scratch_shapes=[sem((2 * batch + 2,))],
            compiler_params=pltpu.CompilerParams(vmem_limit_bytes=60 * 2**20),
        )(*outs)
        return (*arrays, lipschitz.reshape(()), norm_trace)

    placed = (
        P("rep", "rows", "cols", None),
        P("rep", "rows", "cols", None),
        P(),
        P("rows", "cols", None),
    )
    return jax.shard_map(
        per_device,
        mesh=mesh,
        in_specs=placed,
        out_specs=(
            P("rep", "rows", "cols", None),
            P("rep", "rows", "cols", None),
            P(("rows", "cols"), None),
            P("rows", "cols", None),
            P(),
            P(),
        ),
        check_vma=False,
    )
```

```python
import functools
import math

import jax
import jax.numpy as jnp
from jax import lax
from jax.experimental import pallas as pl
from jax.experimental.pallas import tpu as pltpu
from jax.sharding import PartitionSpec as P

MESH = pl.DeviceIdType.MESH
ITERS = 4
F32 = jnp.float32
BF16 = jnp.bfloat16
SIDES = [(v, h) for v in (-1, 0, 1) for h in (-1, 0, 1) if (v, h) != (0, 0)]


def split_rows(rows):
    for block in (13, 11, 10, 9, 8, 7, 6, 5, 4, 3, 2):
        if rows % block == 0:
            return block
    return 1


def kernel(
    nr, nc, counts, in_hbm, up_hbm, k_hbm, p_hbm,
    o_hbm, g_hbm, kg_ref, po_ref, sc_ref,
    in_ref, up_ref, k_ref, p_ref, o_ref, g_ref, load, store,
    fs_row, fr_row, fs_col, fr_col, fs_cor, fr_cor,
    pb, pr_row, ps_col, pr_col, ps_cor, pr_cor,
    xin, xup, xa, xb, wt, ut, gb, r0, h1, r1, h2, r2, h3, r3, tab, yh,
    f_send, f_recv, p_send, p_recv, s0, s1s, s1r, s2s, s2r, s3, ts, tr, sa, sy,
):
    batch, height, breadth, ch = in_ref.shape
    halo = 2 * ITERS
    wide = breadth + 2 * halo
    cell_count, grad_scale = counts
    loads = [
        pltpu.make_async_copy(src, dst, load.at[i])
        for i, (src, dst) in enumerate(
            ((in_hbm, in_ref), (up_hbm, up_ref), (p_hbm, p_ref), (k_hbm, k_ref))
        )
    ]
    stores = [
        pltpu.make_async_copy(src, dst, store.at[i])
        for i, (src, dst) in enumerate(((o_ref, o_hbm), (g_ref, g_hbm)))
    ]
    for one in loads:
        one.start()
    n = nr * nc
    half = nc // 2
    own_rows = height // 2
    ri, ci, rp = lax.axis_index("rows"), lax.axis_index("cols"), lax.axis_index("rep")
    me = ri * nc + ci
    core, cy = lax.rem(ci, 2), ci // 2

    def dev(row, col, rep):
        return {"rows": row, "cols": col, "rep": rep}

    barrier = pltpu.get_barrier_semaphore()

    def greet(k, c):
        t = lax.rem(me + k, n)
        pl.semaphore_signal(
            barrier, inc=1, device_id=dev(t // nc, lax.rem(t, nc), rp), device_id_type=MESH
        )
        return c

    lax.fori_loop(1, n, greet, 0)
    pl.semaphore_signal(barrier, inc=1, device_id=dev(ri, ci, 1 - rp), device_id_type=MESH)

    for f, ref in ((0, in_ref), (1, up_ref)):
        lo = f * batch
        loads[f].wait()
        for s, row in ((0, 0), (1, height - 1)):
            fs_row[s, lo : lo + batch] = ref[:, row]
        for b in range(batch):
            x = ref[b].astype(F32)
            left, right = x[:, 0, :], x[:, breadth - 1, :]
            fs_col[0, lo + b] = left.astype(BF16)
            fs_col[1, lo + b] = right.astype(BF16)
            for h, edge in ((0, left), (1, right)):
                fs_cor[0, h, lo + b] = jnp.broadcast_to(edge[0:1], (16, ch)).astype(BF16)
                fs_cor[1, h, lo + b] = jnp.broadcast_to(
                    edge[height - 1 : height], (16, ch)
                ).astype(BF16)
    loads[2].wait()
    pb[...] = p_ref[...].astype(BF16)
    sent_row = (height - halo) * (1 - rp)
    for h, col in ((0, 0), (1, breadth - halo)):
        edge = p_ref[:, col : col + halo, :]
        ps_col[h] = edge.reshape(height * halo // 16, 16, ch).astype(BF16)
        edge = p_ref[pl.ds(sent_row, halo), col : col + halo, :]
        ps_cor[h] = edge.reshape(halo * halo // 16, 16, ch).astype(BF16)

    pl.semaphore_wait(barrier, n)

    def sidx(v):
        return 0 if v < 0 else 1

    def exists(v, h):
        ok = None
        for d, pos, size in ((v, ri, nr), (h, ci, nc)):
            if d:
                here = (pos > 0) if d < 0 else (pos < size - 1)
                ok = here if ok is None else jnp.logical_and(ok, here)
        return ok

    def target(v, h):
        return dev(lax.rem(ri + v + nr, nr), lax.rem(ci + h + nc, nc), rp)

    def buffers(v, h, row, col, cor):
        if h == 0:
            return row.at[sidx(v)]
        if v == 0:
            return col.at[sidx(h)]
        return cor.at[sidx(v), sidx(h)]

    def f_copy(k):
        v, h = SIDES[k]
        return pltpu.make_async_remote_copy(
            src_ref=buffers(v, h, fs_row, fs_col, fs_cor),
            dst_ref=buffers(-v, -h, fr_row, fr_col, fr_cor),
            send_sem=f_send.at[k],
            recv_sem=f_recv.at[k],
            device_id=target(v, h),
            device_id_type=MESH,
        )

    def p_copy(k):
        h = (0, -1, 1, -1, 1)[k]
        if k == 0:
            src, dst = pb.at[pl.ds(sent_row, halo)], pr_row
        elif k < 3:
            src, dst = ps_cor.at[sidx(h)], pr_cor.at[sidx(-h)]
        else:
            src, dst = ps_col.at[sidx(h)], pr_col.at[sidx(-h)]
        row = lax.rem(ri + 1 - 2 * rp + nr, nr) if k < 3 else ri
        return pltpu.make_async_remote_copy(
            src_ref=src,
            dst_ref=dst,
            send_sem=p_send.at[k],
            recv_sem=p_recv.at[k],
            device_id=dev(row, lax.rem(ci + h + nc, nc), rp),
            device_id_type=MESH,
        )

    for k, (v, h) in enumerate(SIDES):
        @pl.when(exists(v, h))
        def _(k=k):
            f_copy(k).start()

        @pl.when(jnp.logical_not(exists(v, h)))
        def _(v=v, h=h):
            ref = buffers(v, h, fr_row, fr_col, fr_cor)
            ref[...] = jnp.zeros(ref.shape, BF16)

    for k in range(5):
        p_copy(k).start()

    loads[3].wait()

    for a in range(3):
        for b in range(3):
            wt[a, b * ch : (b + 1) * ch, :] = k_ref[2 - a, 2 - b].T
    cells = height * breadth

    def turn(b, c):
        ut[:, pl.ds(pl.multiple_of(b * cells, 128), cells)] = (
            up_ref[b].reshape(cells, ch).T
        )
        return c

    lax.fori_loop(0, batch, turn, 0)

    for k, (v, h) in enumerate(SIDES):
        @pl.when(exists(-v, -h))
        def _(k=k):
            f_copy(k).wait_recv()

    def put_padded(dst, b, row, value, lefts, rights):
        rows = value.shape[0]
        flat = value.reshape(rows * breadth, ch)
        j = lax.broadcasted_iota(jnp.int32, (rows, breadth, ch), 1)
        left = pltpu.roll(flat, 1, 0).reshape(rows, breadth, ch)
        right = pltpu.roll(flat, rows * breadth - 1, 0).reshape(rows, breadth, ch)
        left = jnp.where(j == 0, lefts[:, None, :], left)
        right = jnp.where(j == breadth - 1, rights[:, None, :], right)
        dst[b, row : row + rows, :, 0:ch] = left.astype(BF16)
        dst[b, row : row + rows, :, ch : 2 * ch] = value.astype(BF16)
        dst[b, row : row + rows, :, 2 * ch :] = right.astype(BF16)

    def pad_fields(f, ref, dst):
        def step(b, c):
            e = f * batch + b
            put_padded(
                dst, b, 1, ref[b].astype(F32),
                fr_col[0, e].astype(F32), fr_col[1, e].astype(F32),
            )
            for s, row in ((0, 0), (1, height + 1)):
                put_padded(
                    dst, b, row, fr_row[s, e].astype(F32)[None],
                    fr_cor[s, 0, e].astype(F32)[0:1], fr_cor[s, 1, e].astype(F32)[0:1],
                )
            return c

        lax.fori_loop(0, batch, step, 0)

    pad_fields(0, in_ref, xin)

    dper = ch // n

    def grad_step(a, c):
        for b in range(3):
            window = xin[:, pl.ds(a, height), :, b * ch : (b + 1) * ch]
            acc = jnp.dot(
                ut[...], window.reshape(batch * cells, ch), preferred_element_type=F32
            )
            at = pl.multiple_of(a * (3 * ch) + b * ch, 128)
            for t in range(n):
                rr, cc = t // nc, t % nc
                gb[cc % 2, cc // 2, rr, :, pl.ds(at, ch)] = acc[
                    t * dper : (t + 1) * dper
                ].astype(BF16)
        return c

    lax.fori_loop(0, 3, grad_step, 0)

    def copy0():
        return pltpu.make_async_remote_copy(
            src_ref=gb.at[1 - core],
            dst_ref=r0,
            send_sem=s0.at[0],
            recv_sem=s0.at[1],
            device_id=dev(ri, ci + 1 - 2 * core, rp),
            device_id_type=MESH,
        )

    def copy1(k):
        to = lax.rem(cy + k, half)
        return pltpu.make_async_remote_copy(
            src_ref=h1.at[to],
            dst_ref=r1.at[k - 1],
            send_sem=s1s.at[k - 1],
            recv_sem=s1r.at[k - 1],
            device_id=dev(ri, to * 2 + core, rp),
            device_id_type=MESH,
        )

    def copy2(k):
        to = lax.rem(ri + k, nr)
        return pltpu.make_async_remote_copy(
            src_ref=h2.at[to],
            dst_ref=r2.at[k - 1],
            send_sem=s2s.at[k - 1],
            recv_sem=s2r.at[k - 1],
            device_id=dev(to, ci, rp),
            device_id_type=MESH,
        )

    def copy3():
        return pltpu.make_async_remote_copy(
            src_ref=h3,
            dst_ref=r3,
            send_sem=s3.at[0],
            recv_sem=s3.at[1],
            device_id=dev(ri, ci, 1 - rp),
            device_id_type=MESH,
        )

    copy0().start()

    def field_conv(src, dst, weights, begin, end):
        block = min(height, 8)

        def step(t, c):
            b, row = t // (height // block), lax.rem(t, height // block) * block
            windows = [
                src[b, pl.ds(row + a, block)].reshape(block * breadth, 3 * ch)
                for a in range(3)
            ]
            acc = jnp.dot(
                jnp.concatenate(windows, axis=1), weights(), preferred_element_type=F32
            )
            dst[b, pl.ds(row, block)] = acc.reshape(block, breadth, ch).astype(BF16)
            return c

        lax.fori_loop(
            begin * (height // block), end * (height // block), step, 0
        )

    def forward():
        return k_ref[...].reshape(9 * ch, ch)

    def adjoint():
        return wt[...].reshape(9 * ch, ch)

    field_conv(xin, o_ref, forward, 0, batch)
    stores[0].start()

    copy0().wait_recv()

    def sum0(t, c):
        a, b = t // nr, lax.rem(t, nr)
        h1[a, b] = (gb[core, a, b].astype(F32) + r0[a, b].astype(F32)).astype(BF16)
        return c

    lax.fori_loop(0, half * nr, sum0, 0)
    for k in range(1, half):
        copy1(k).start()

    pad_fields(1, up_ref, xup)

    def put(dst, row, value):
        rows = value.shape[0]
        flat = value.reshape(rows * wide, ch)
        left = pltpu.roll(flat, 1, 0)
        right = pltpu.roll(flat, rows * wide - 1, 0)
        dst[pl.ds(row, rows), :, 0:ch] = left.reshape(rows, wide, ch).astype(BF16)
        dst[pl.ds(row, rows), :, ch : 2 * ch] = value.astype(BF16)
        dst[pl.ds(row, rows), :, 2 * ch :] = right.reshape(rows, wide, ch).astype(BF16)

    for k in range(5):
        p_copy(k).wait_recv()
    put(
        xa, rp * height,
        jnp.concatenate(
            [
                pr_cor[0].astype(F32).reshape(halo, halo, ch),
                pr_row[...].astype(F32),
                pr_cor[1].astype(F32).reshape(halo, halo, ch),
            ],
            axis=1,
        ),
    )
    put(
        xa, halo * (1 - rp),
        jnp.concatenate(
            [
                pr_col[0].astype(F32).reshape(height, halo, ch),
                pb[...].astype(F32),
                pr_col[1].astype(F32).reshape(height, halo, ch),
            ],
            axis=1,
        ),
    )

    def tile_conv(src, row, block, weights):
        windows = [
            src[pl.ds(row + a, block)].reshape(block * wide, 3 * ch) for a in range(3)
        ]
        return jnp.dot(
            jnp.concatenate(windows, axis=1), weights(), preferred_element_type=F32
        )

    def fold(x):
        return jnp.sum(x.reshape(-1, 8, ch), axis=0)

    def total(x):
        return jnp.sum(jnp.sum(x, axis=0, keepdims=True), axis=1, keepdims=True)

    def note(row, value):
        tab[me, rp, row : row + 1, :] = jnp.broadcast_to(value, (1, 128))

    factor = None
    rows = own_rows + 2 * halo
    for it in range(ITERS):
        rows -= 2
        block = split_rows(rows)

        def ahead(t, c, block=block, factor=factor):
            acc = tile_conv(xa, t * block, block, forward)
            if factor is not None:
                acc = acc * factor
            put(xb, t * block, acc.reshape(block, wide, ch))
            return c

        lax.fori_loop(0, rows // block, ahead, 0)
        rows -= 2
        block = split_rows(rows)
        first = (rows - own_rows) // 2
        last = it + 1 == ITERS

        def back(t, c, block=block, first=first, last=last):
            own, every, rounded = c
            acc = tile_conv(xb, t * block, block, adjoint)
            full = acc.reshape(block, wide, ch)
            mine = full[:, halo : halo + breadth, :]
            if last:
                yh[rp, pl.ds(t * block, block)] = mine.astype(BF16)
                return own + fold(mine * mine), every, rounded
            put(xa, t * block, full)
            where = t * block + lax.broadcasted_iota(jnp.int32, mine.shape, 0)
            inside = jnp.logical_and(where >= first, where < first + own_rows)
            mine = jnp.where(inside, mine, 0.0)
            near = mine.astype(BF16).astype(F32)
            return (
                own + fold(mine * mine),
                every + fold(acc * acc),
                rounded + fold(near * near),
            )

        zero = jnp.zeros((8, ch), F32)
        own, every, rounded = lax.fori_loop(0, rows // block, back, (zero, zero, zero))
        note(it, total(own))
        if it == ITERS - 2:
            note(ITERS, total(rounded))
        if not last:
            mean = total(every) / float(rows * wide * ch)
            root = jnp.sqrt(jnp.maximum(mean, 1e-30))
            factor = 1.0 / root
            note(ITERS + 1 + it, root)
        if it == 1:
            for k in range(1, half):
                copy1(k).wait_recv()

            def sum1(b, c):
                acc = h1[cy, b].astype(F32)
                for k in range(1, half):
                    acc = acc + r1[k - 1, b].astype(F32)
                h2[b] = acc.astype(BF16)
                return c

            lax.fori_loop(0, nr, sum1, 0)
            for k in range(1, nr):
                copy2(k).start()
    def copya():
        return pltpu.make_async_remote_copy(
            src_ref=tab.at[me, rp],
            dst_ref=tab.at[me, rp],
            send_sem=sa.at[0],
            recv_sem=sa.at[1],
            device_id=dev(ri, ci, 1 - rp),
            device_id_type=MESH,
        )

    def copyy():
        return pltpu.make_async_remote_copy(
            src_ref=yh.at[rp],
            dst_ref=yh.at[rp],
            send_sem=sy.at[0],
            recv_sem=sy.at[1],
            device_id=dev(ri, ci, 1 - rp),
            device_id_type=MESH,
        )

    copya().start()
    copyy().start()

    def copyt(k):
        to = lax.rem(me + k, n)
        return pltpu.make_async_remote_copy(
            src_ref=tab.at[me],
            dst_ref=tab.at[me],
            send_sem=ts.at[k],
            recv_sem=tr.at[k],
            device_id=dev(to // nc, lax.rem(to, nc), rp),
            device_id_type=MESH,
        )

    def copyt_in(k):
        of = lax.rem(me - k + n, n)
        return pltpu.make_async_remote_copy(
            src_ref=tab.at[me],
            dst_ref=tab.at[of],
            send_sem=ts.at[k],
            recv_sem=tr.at[k],
            device_id=dev(of // nc, lax.rem(of, nc), rp),
            device_id_type=MESH,
        )

    def tell(k, c):
        copyt(k).start()
        return c

    field_conv(xup, g_ref, adjoint, 0, batch // 2)
    copya().wait_recv()
    lax.fori_loop(1, n, tell, 0)
    for k in range(1, nr):
        copy2(k).wait_recv()
    acc = h2[ri].astype(F32)
    for k in range(1, nr):
        acc = acc + r2[k - 1].astype(F32)
    h3[...] = acc.astype(BF16)
    copy3().start()
    field_conv(xup, g_ref, adjoint, batch // 2, batch)
    stores[1].start()

    def hear(k, c):
        copyt_in(k).wait_recv()
        return c

    lax.fori_loop(1, n, hear, 0)
    told = tab[...].reshape(2 * n, 8, 128)
    gain = jnp.ones((2 * n, 128), F32)
    for it in range(ITERS - 1):
        squared = jnp.sum(told[:, it, :] * gain * gain, axis=0, keepdims=True)
        scale = jnp.sqrt(squared / cell_count + 1e-06)
        sc_ref[it + 1 : it + 2, :] = scale
        gain = gain / scale
        if it == ITERS - 2:
            sum_probe = jnp.sum(told[:, ITERS, :] * gain * gain, axis=0, keepdims=True)
        gain = gain * told[:, ITERS + 1 + it, :]
    sum_back = jnp.sum(told[:, ITERS - 1, :] * gain * gain, axis=0, keepdims=True)
    sc_ref[0:1, :] = jnp.sqrt(jnp.sqrt(sum_back / sum_probe))
    copyy().wait_recv()
    for q in range(2):
        own_gain = 1.0 / jnp.sqrt(sum_back / cell_count + 1e-06)
        for it in range(ITERS - 1):
            own_gain = own_gain * tab[me, q, ITERS + 1 + it : ITERS + 2 + it, :]
            own_gain = own_gain / sc_ref[it + 1 : it + 2, :]
        both = jnp.concatenate([own_gain] * (ch // 128), axis=1).reshape(1, 1, ch)
        po_ref[q * own_rows : (q + 1) * own_rows] = yh[q].astype(F32) * both

    copy3().wait_recv()
    kg_ref[...] = (h3[...].astype(F32) + r3[...].astype(F32)) * grad_scale

    for k, (v, h) in enumerate(SIDES):
        @pl.when(exists(v, h))
        def _(k=k):
            f_copy(k).wait_send()

    for k in range(5):
        p_copy(k).wait_send()
    copya().wait_send()
    copyy().wait_send()
    copy0().wait_send()
    for k in range(1, half):
        copy1(k).wait_send()
    for k in range(1, nr):
        copy2(k).wait_send()
    copy3().wait_send()

    for one in stores:
        one.wait()

    def sent(k, c):
        copyt(k).wait_send()
        return c

    lax.fori_loop(1, n, sent, 0)


def finish(
    o_in, g_in, kg_in, po_in, sc_in, o_out, g_out, kg_out, po_out, lip, trace,
    o_mid, g_mid, kg_mid, po_mid, in_sems, out_sems,
):
    parts = []
    for a in range(o_in.shape[0]):
        parts.append((o_in.at[a], o_mid.at[a], o_out.at[a]))
        parts.append((g_in.at[a], g_mid.at[a], g_out.at[a]))
    parts.append((po_in, po_mid, po_out))
    parts.append((kg_in, kg_mid, kg_out))
    inward = [
        pltpu.make_async_copy(src, mid, in_sems.at[i]) for i, (src, mid, _) in enumerate(parts)
    ]
    outward = [
        pltpu.make_async_copy(mid, dst, out_sems.at[i]) for i, (_, mid, dst) in enumerate(parts)
    ]
    for one in inward:
        one.start()
    lip[0] = sc_in[0, 0]
    for i in range(ITERS - 1):
        trace[i] = sc_in[i + 1, 0]
    for one, two in zip(inward, outward):
        one.wait()
        two.start()
    for two in outward:
        two.wait()


def solution(mesh):
    nr, nc = mesh.shape["rows"], mesh.shape["cols"]
    reps = mesh.shape["rep"]

    def per_device(inputs, upstream, weights, probe_init):
        batch, height, breadth, ch = inputs.shape
        n = nr * nc
        half = nc // 2
        dper = ch // n
        halo = 2 * ITERS
        wide = breadth + 2 * halo
        cell_count = float(height * nr * breadth * nc * ch)
        grad_scale = 1.0 / math.sqrt(batch * reps * height * nr * breadth * nc)
        cells = height * breadth
        sem = pltpu.SemaphoreType.DMA
        vmem = pl.BlockSpec(memory_space=pltpu.VMEM)
        scratch = [
            ((2, 2 * batch, breadth, ch), BF16),
            ((2, 2 * batch, breadth, ch), BF16),
            ((2, 2 * batch, height, ch), BF16),
            ((2, 2 * batch, height, ch), BF16),
            ((2, 2, 2 * batch, 16, ch), BF16),
            ((2, 2, 2 * batch, 16, ch), BF16),
            ((height, breadth, ch), BF16),
            ((halo, breadth, ch), BF16),
            ((2, height * halo // 16, 16, ch), BF16),
            ((2, height * halo // 16, 16, ch), BF16),
            ((2, halo * halo // 16, 16, ch), BF16),
            ((2, halo * halo // 16, 16, ch), BF16),
            ((batch, height + 2, breadth, 3 * ch), BF16),
            ((batch, height + 2, breadth, 3 * ch), BF16),
            ((height + halo, wide, 3 * ch), BF16),
            ((height + halo, wide, 3 * ch), BF16),
            ((3, 3 * ch, ch), BF16),
            ((ch, batch * cells), BF16),
            ((2, half, nr, dper, 9 * ch), BF16),
            ((half, nr, dper, 9 * ch), BF16),
            ((half, nr, dper, 9 * ch), BF16),
            ((half - 1, nr, dper, 9 * ch), BF16),
            ((nr, dper, 9 * ch), BF16),
            ((nr - 1, dper, 9 * ch), BF16),
            ((dper, 9 * ch), BF16),
            ((dper, 9 * ch), BF16),
            ((n, 2, 8, 128), F32),
            ((2, height // 2, breadth, ch), BF16),
        ]
        anywhere = pl.BlockSpec(memory_space=pl.ANY)
        staged = [
            (inputs.shape, BF16), (inputs.shape, BF16), (weights.shape, BF16),
            (probe_init.shape, F32), (inputs.shape, BF16), (inputs.shape, BF16),
        ]
        outs = pl.pallas_call(
            functools.partial(kernel, nr, nc, (cell_count, grad_scale)),
            out_shape=(
                jax.ShapeDtypeStruct(inputs.shape, BF16),
                jax.ShapeDtypeStruct(inputs.shape, BF16),
                jax.ShapeDtypeStruct((dper, 9 * ch), F32),
                jax.ShapeDtypeStruct(probe_init.shape, F32),
                jax.ShapeDtypeStruct((8, 128), F32),
            ),
            in_specs=[anywhere] * 4,
            out_specs=[anywhere] * 2 + [vmem] * 3,
            scratch_shapes=[pltpu.VMEM(s, t) for s, t in staged]
            + [sem((4,)), sem((2,))]
            + [pltpu.VMEM(s, t) for s, t in scratch]
            + [
                sem((8,)), sem((8,)), sem((5,)), sem((5,)), sem((2,)),
                sem((max(half - 1, 1),)), sem((max(half - 1, 1),)),
                sem((nr - 1,)), sem((nr - 1,)), sem((2,)), sem((n,)), sem((n,)),
                sem((2,)), sem((2,)),
            ],
            compiler_params=pltpu.CompilerParams(
                collective_id=0, has_side_effects=True, vmem_limit_bytes=60 * 2**20
            ),
        )(inputs, upstream, weights, probe_init)
        smem = pl.BlockSpec(memory_space=pltpu.SMEM)
        *arrays, lipschitz, norm_trace = pl.pallas_call(
            finish,
            out_shape=tuple(jax.ShapeDtypeStruct(x.shape, x.dtype) for x in outs[:4])
            + (jax.ShapeDtypeStruct((1,), F32), jax.ShapeDtypeStruct((ITERS - 1,), F32)),
            in_specs=[anywhere] * 4 + [smem],
            out_specs=[anywhere] * 4 + [smem] * 2,
            scratch_shapes=[pltpu.VMEM(x.shape, x.dtype) for x in outs[:4]]
            + [sem((2 * batch + 2,)), sem((2 * batch + 2,))],
            compiler_params=pltpu.CompilerParams(vmem_limit_bytes=60 * 2**20),
        )(*outs)
        return (*arrays, lipschitz.reshape(()), norm_trace)

    placed = (
        P("rep", "rows", "cols", None),
        P("rep", "rows", "cols", None),
        P(),
        P("rows", "cols", None),
    )
    return jax.shard_map(
        per_device,
        mesh=mesh,
        in_specs=placed,
        out_specs=(
            P("rep", "rows", "cols", None),
            P("rep", "rows", "cols", None),
            P(("rows", "cols"), None),
            P("rows", "cols", None),
            P(),
            P(),
        ),
        check_vma=False,
    )
```

```python
import functools
import math

import jax
import jax.numpy as jnp
from jax import lax
from jax.experimental import pallas as pl
from jax.experimental.pallas import tpu as pltpu
from jax.sharding import PartitionSpec as P

MESH = pl.DeviceIdType.MESH
ITERS = 4
F32 = jnp.float32
BF16 = jnp.bfloat16
SIDES = [(v, h) for v in (-1, 0, 1) for h in (-1, 0, 1) if (v, h) != (0, 0)]


def split_rows(rows):
    for block in (13, 11, 10, 9, 8, 7, 6, 5, 4, 3, 2):
        if rows % block == 0:
            return block
    return 1


def kernel(
    nr, nc, counts, in_hbm, up_hbm, k_hbm, p_hbm,
    o_hbm, g_hbm, kg_ref, po_ref, sc_ref,
    in_ref, up_ref, k_ref, p_ref, o_ref, g_ref, load, store,
    fs_row, fr_row, fs_col, fr_col, fs_cor, fr_cor,
    pb, pr_row, ps_col, pr_col, ps_cor, pr_cor,
    xin, xup, xa, xb, wt, ut, gb, r0, h1, r1, h2, r2, h3, r3, tab, yh,
    f_send, f_recv, p_send, p_recv, s0, s1s, s1r, s2s, s2r, s3, ts, tr, sa, sy,
):
    batch, height, breadth, ch = in_ref.shape
    halo = 2 * ITERS
    wide = breadth + 2 * halo
    cell_count, grad_scale = counts
    loads = [
        pltpu.make_async_copy(src, dst, load.at[i])
        for i, (src, dst) in enumerate(
            ((in_hbm, in_ref), (up_hbm, up_ref), (p_hbm, p_ref), (k_hbm, k_ref))
        )
    ]
    stores = [
        pltpu.make_async_copy(src, dst, store.at[i])
        for i, (src, dst) in enumerate(((o_ref, o_hbm), (g_ref, g_hbm)))
    ]
    for one in loads:
        one.start()
    n = nr * nc
    half = nc // 2
    own_rows = height // 2
    ri, ci, rp = lax.axis_index("rows"), lax.axis_index("cols"), lax.axis_index("rep")
    me = ri * nc + ci
    core, cy = lax.rem(ci, 2), ci // 2

    def dev(row, col, rep):
        return {"rows": row, "cols": col, "rep": rep}

    barrier = pltpu.get_barrier_semaphore()

    def greet(k, c):
        t = lax.rem(me + k, n)
        pl.semaphore_signal(
            barrier, inc=1, device_id=dev(t // nc, lax.rem(t, nc), rp), device_id_type=MESH
        )
        return c

    lax.fori_loop(1, n, greet, 0)
    pl.semaphore_signal(barrier, inc=1, device_id=dev(ri, ci, 1 - rp), device_id_type=MESH)

    for f, ref in ((0, in_ref), (1, up_ref)):
        lo = f * batch
        loads[f].wait()
        for s, row in ((0, 0), (1, height - 1)):
            fs_row[s, lo : lo + batch] = ref[:, row]
        for b in range(batch):
            x = ref[b].astype(F32)
            left, right = x[:, 0, :], x[:, breadth - 1, :]
            fs_col[0, lo + b] = left.astype(BF16)
            fs_col[1, lo + b] = right.astype(BF16)
            for h, edge in ((0, left), (1, right)):
                fs_cor[0, h, lo + b] = jnp.broadcast_to(edge[0:1], (16, ch)).astype(BF16)
                fs_cor[1, h, lo + b] = jnp.broadcast_to(
                    edge[height - 1 : height], (16, ch)
                ).astype(BF16)
    loads[2].wait()
    pb[...] = p_ref[...].astype(BF16)
    sent_row = (height - halo) * (1 - rp)
    for h, col in ((0, 0), (1, breadth - halo)):
        edge = p_ref[:, col : col + halo, :]
        ps_col[h] = edge.reshape(height * halo // 16, 16, ch).astype(BF16)
        edge = p_ref[pl.ds(sent_row, halo), col : col + halo, :]
        ps_cor[h] = edge.reshape(halo * halo // 16, 16, ch).astype(BF16)

    pl.semaphore_wait(barrier, n)

    def sidx(v):
        return 0 if v < 0 else 1

    def exists(v, h):
        ok = None
        for d, pos, size in ((v, ri, nr), (h, ci, nc)):
            if d:
                here = (pos > 0) if d < 0 else (pos < size - 1)
                ok = here if ok is None else jnp.logical_and(ok, here)
        return ok

    def target(v, h):
        return dev(lax.rem(ri + v + nr, nr), lax.rem(ci + h + nc, nc), rp)

    def buffers(v, h, row, col, cor):
        if h == 0:
            return row.at[sidx(v)]
        if v == 0:
            return col.at[sidx(h)]
        return cor.at[sidx(v), sidx(h)]

    def f_copy(k):
        v, h = SIDES[k]
        return pltpu.make_async_remote_copy(
            src_ref=buffers(v, h, fs_row, fs_col, fs_cor),
            dst_ref=buffers(-v, -h, fr_row, fr_col, fr_cor),
            send_sem=f_send.at[k],
            recv_sem=f_recv.at[k],
            device_id=target(v, h),
            device_id_type=MESH,
        )

    def p_copy(k):
        h = (0, -1, 1, -1, 1)[k]
        if k == 0:
            src, dst = pb.at[pl.ds(sent_row, halo)], pr_row
        elif k < 3:
            src, dst = ps_cor.at[sidx(h)], pr_cor.at[sidx(-h)]
        else:
            src, dst = ps_col.at[sidx(h)], pr_col.at[sidx(-h)]
        row = lax.rem(ri + 1 - 2 * rp + nr, nr) if k < 3 else ri
        return pltpu.make_async_remote_copy(
            src_ref=src,
            dst_ref=dst,
            send_sem=p_send.at[k],
            recv_sem=p_recv.at[k],
            device_id=dev(row, lax.rem(ci + h + nc, nc), rp),
            device_id_type=MESH,
        )

    for k, (v, h) in enumerate(SIDES):
        @pl.when(exists(v, h))
        def _(k=k):
            f_copy(k).start()

        @pl.when(jnp.logical_not(exists(v, h)))
        def _(v=v, h=h):
            ref = buffers(v, h, fr_row, fr_col, fr_cor)
            ref[...] = jnp.zeros(ref.shape, BF16)

    for k in range(5):
        p_copy(k).start()

    loads[3].wait()

    for a in range(3):
        for b in range(3):
            wt[a, b * ch : (b + 1) * ch, :] = k_ref[2 - a, 2 - b].T
    cells = height * breadth

    def turn(b, c):
        ut[:, pl.ds(pl.multiple_of(b * cells, 128), cells)] = (
            up_ref[b].reshape(cells, ch).T
        )
        return c

    lax.fori_loop(0, batch, turn, 0)

    for k, (v, h) in enumerate(SIDES):
        @pl.when(exists(-v, -h))
        def _(k=k):
            f_copy(k).wait_recv()

    def put_padded(dst, b, row, value, lefts, rights):
        rows = value.shape[0]
        flat = value.reshape(rows * breadth, ch)
        j = lax.broadcasted_iota(jnp.int32, (rows, breadth, ch), 1)
        left = pltpu.roll(flat, 1, 0).reshape(rows, breadth, ch)
        right = pltpu.roll(flat, rows * breadth - 1, 0).reshape(rows, breadth, ch)
        left = jnp.where(j == 0, lefts[:, None, :], left)
        right = jnp.where(j == breadth - 1, rights[:, None, :], right)
        dst[b, row : row + rows, :, 0:ch] = left.astype(BF16)
        dst[b, row : row + rows, :, ch : 2 * ch] = value.astype(BF16)
        dst[b, row : row + rows, :, 2 * ch :] = right.astype(BF16)

    def pad_fields(f, ref, dst):
        def step(b, c):
            e = f * batch + b
            put_padded(
                dst, b, 1, ref[b].astype(F32),
                fr_col[0, e].astype(F32), fr_col[1, e].astype(F32),
            )
            for s, row in ((0, 0), (1, height + 1)):
                put_padded(
                    dst, b, row, fr_row[s, e].astype(F32)[None],
                    fr_cor[s, 0, e].astype(F32)[0:1], fr_cor[s, 1, e].astype(F32)[0:1],
                )
            return c

        lax.fori_loop(0, batch, step, 0)

    pad_fields(0, in_ref, xin)

    dper = ch // n

    def grad_step(a, c):
        for b in range(3):
            window = xin[:, pl.ds(a, height), :, b * ch : (b + 1) * ch]
            acc = jnp.dot(
                ut[...], window.reshape(batch * cells, ch), preferred_element_type=F32
            )
            at = pl.multiple_of(a * (3 * ch) + b * ch, 128)
            for t in range(n):
                rr, cc = t // nc, t % nc
                gb[cc % 2, cc // 2, rr, :, pl.ds(at, ch)] = acc[
                    t * dper : (t + 1) * dper
                ].astype(BF16)
        return c

    lax.fori_loop(0, 3, grad_step, 0)

    def copy0():
        return pltpu.make_async_remote_copy(
            src_ref=gb.at[1 - core],
            dst_ref=r0,
            send_sem=s0.at[0],
            recv_sem=s0.at[1],
            device_id=dev(ri, ci + 1 - 2 * core, rp),
            device_id_type=MESH,
        )

    def copy1(k):
        to = lax.rem(cy + k, half)
        return pltpu.make_async_remote_copy(
            src_ref=h1.at[to],
            dst_ref=r1.at[k - 1],
            send_sem=s1s.at[k - 1],
            recv_sem=s1r.at[k - 1],
            device_id=dev(ri, to * 2 + core, rp),
            device_id_type=MESH,
        )

    def copy2(k):
        to = lax.rem(ri + k, nr)
        return pltpu.make_async_remote_copy(
            src_ref=h2.at[to],
            dst_ref=r2.at[k - 1],
            send_sem=s2s.at[k - 1],
            recv_sem=s2r.at[k - 1],
            device_id=dev(to, ci, rp),
            device_id_type=MESH,
        )

    def copy3():
        return pltpu.make_async_remote_copy(
            src_ref=h3,
            dst_ref=r3,
            send_sem=s3.at[0],
            recv_sem=s3.at[1],
            device_id=dev(ri, ci, 1 - rp),
            device_id_type=MESH,
        )

    copy0().start()

    def field_conv(src, dst, weights, begin, end):
        block = min(height, 8)

        def step(t, c):
            b, row = t // (height // block), lax.rem(t, height // block) * block
            windows = [
                src[b, pl.ds(row + a, block)].reshape(block * breadth, 3 * ch)
                for a in range(3)
            ]
            acc = jnp.dot(
                jnp.concatenate(windows, axis=1), weights(), preferred_element_type=F32
            )
            dst[b, pl.ds(row, block)] = acc.reshape(block, breadth, ch).astype(BF16)
            return c

        lax.fori_loop(
            begin * (height // block), end * (height // block), step, 0
        )

    def forward():
        return k_ref[...].reshape(9 * ch, ch)

    def adjoint():
        return wt[...].reshape(9 * ch, ch)

    field_conv(xin, o_ref, forward, 0, 1)

    copy0().wait_recv()

    def sum0(t, c):
        a, b = t // nr, lax.rem(t, nr)
        h1[a, b] = (gb[core, a, b].astype(F32) + r0[a, b].astype(F32)).astype(BF16)
        return c

    lax.fori_loop(0, half * nr, sum0, 0)
    for k in range(1, half):
        copy1(k).start()

    field_conv(xin, o_ref, forward, 1, batch)
    stores[0].start()
    pad_fields(1, up_ref, xup)

    def put(dst, row, value):
        rows = value.shape[0]
        flat = value.reshape(rows * wide, ch)
        left = pltpu.roll(flat, 1, 0)
        right = pltpu.roll(flat, rows * wide - 1, 0)
        dst[pl.ds(row, rows), :, 0:ch] = left.reshape(rows, wide, ch).astype(BF16)
        dst[pl.ds(row, rows), :, ch : 2 * ch] = value.astype(BF16)
        dst[pl.ds(row, rows), :, 2 * ch :] = right.reshape(rows, wide, ch).astype(BF16)

    for k in range(5):
        p_copy(k).wait_recv()
    put(
        xa, rp * height,
        jnp.concatenate(
            [
                pr_cor[0].astype(F32).reshape(halo, halo, ch),
                pr_row[...].astype(F32),
                pr_cor[1].astype(F32).reshape(halo, halo, ch),
            ],
            axis=1,
        ),
    )
    put(
        xa, halo * (1 - rp),
        jnp.concatenate(
            [
                pr_col[0].astype(F32).reshape(height, halo, ch),
                pb[...].astype(F32),
                pr_col[1].astype(F32).reshape(height, halo, ch),
            ],
            axis=1,
        ),
    )

    def tile_conv(src, row, block, weights):
        windows = [
            src[pl.ds(row + a, block)].reshape(block * wide, 3 * ch) for a in range(3)
        ]
        return jnp.dot(
            jnp.concatenate(windows, axis=1), weights(), preferred_element_type=F32
        )

    def fold(x):
        return jnp.sum(x.reshape(-1, 8, ch), axis=0)

    def total(x):
        return jnp.sum(jnp.sum(x, axis=0, keepdims=True), axis=1, keepdims=True)

    def note(row, value):
        tab[me, rp, row : row + 1, :] = jnp.broadcast_to(value, (1, 128))

    factor = None
    rows = own_rows + 2 * halo
    for it in range(ITERS):
        rows -= 2
        block = split_rows(rows)

        def ahead(t, c, block=block, factor=factor):
            acc = tile_conv(xa, t * block, block, forward)
            if factor is not None:
                acc = acc * factor
            put(xb, t * block, acc.reshape(block, wide, ch))
            return c

        lax.fori_loop(0, rows // block, ahead, 0)
        rows -= 2
        block = split_rows(rows)
        first = (rows - own_rows) // 2
        last = it + 1 == ITERS

        def back(t, c, block=block, first=first, last=last):
            own, every, rounded = c
            acc = tile_conv(xb, t * block, block, adjoint)
            full = acc.reshape(block, wide, ch)
            mine = full[:, halo : halo + breadth, :]
            if last:
                yh[rp, pl.ds(t * block, block)] = mine.astype(BF16)
                return own + fold(mine * mine), every, rounded
            put(xa, t * block, full)
            where = t * block + lax.broadcasted_iota(jnp.int32, mine.shape, 0)
            inside = jnp.logical_and(where >= first, where < first + own_rows)
            mine = jnp.where(inside, mine, 0.0)
            near = mine.astype(BF16).astype(F32)
            return (
                own + fold(mine * mine),
                every + fold(acc * acc),
                rounded + fold(near * near),
            )

        zero = jnp.zeros((8, ch), F32)
        own, every, rounded = lax.fori_loop(0, rows // block, back, (zero, zero, zero))
        note(it, total(own))
        if it == ITERS - 2:
            note(ITERS, total(rounded))
        if not last:
            mean = total(every) / float(rows * wide * ch)
            root = jnp.sqrt(jnp.maximum(mean, 1e-30))
            factor = 1.0 / root
            note(ITERS + 1 + it, root)
        if it == 0:
            for k in range(1, half):
                copy1(k).wait_recv()

            def sum1(b, c):
                acc = h1[cy, b].astype(F32)
                for k in range(1, half):
                    acc = acc + r1[k - 1, b].astype(F32)
                h2[b] = acc.astype(BF16)
                return c

            lax.fori_loop(0, nr, sum1, 0)
            for k in range(1, nr):
                copy2(k).start()
    def copya():
        return pltpu.make_async_remote_copy(
            src_ref=tab.at[me, rp],
            dst_ref=tab.at[me, rp],
            send_sem=sa.at[0],
            recv_sem=sa.at[1],
            device_id=dev(ri, ci, 1 - rp),
            device_id_type=MESH,
        )

    def copyy():
        return pltpu.make_async_remote_copy(
            src_ref=yh.at[rp],
            dst_ref=yh.at[rp],
            send_sem=sy.at[0],
            recv_sem=sy.at[1],
            device_id=dev(ri, ci, 1 - rp),
            device_id_type=MESH,
        )

    copya().start()
    copyy().start()

    def copyt(k):
        to = lax.rem(me + k, n)
        return pltpu.make_async_remote_copy(
            src_ref=tab.at[me],
            dst_ref=tab.at[me],
            send_sem=ts.at[k],
            recv_sem=tr.at[k],
            device_id=dev(to // nc, lax.rem(to, nc), rp),
            device_id_type=MESH,
        )

    def copyt_in(k):
        of = lax.rem(me - k + n, n)
        return pltpu.make_async_remote_copy(
            src_ref=tab.at[me],
            dst_ref=tab.at[of],
            send_sem=ts.at[k],
            recv_sem=tr.at[k],
            device_id=dev(of // nc, lax.rem(of, nc), rp),
            device_id_type=MESH,
        )

    def tell(k, c):
        copyt(k).start()
        return c

    field_conv(xup, g_ref, adjoint, 0, 1)
    copya().wait_recv()
    lax.fori_loop(1, n, tell, 0)
    for k in range(1, nr):
        copy2(k).wait_recv()
    acc = h2[ri].astype(F32)
    for k in range(1, nr):
        acc = acc + r2[k - 1].astype(F32)
    h3[...] = acc.astype(BF16)
    copy3().start()
    field_conv(xup, g_ref, adjoint, 1, batch)
    stores[1].start()

    def hear(k, c):
        copyt_in(k).wait_recv()
        return c

    lax.fori_loop(1, n, hear, 0)
    told = tab[...].reshape(2 * n, 8, 128)
    gain = jnp.ones((2 * n, 128), F32)
    for it in range(ITERS - 1):
        squared = jnp.sum(told[:, it, :] * gain * gain, axis=0, keepdims=True)
        scale = jnp.sqrt(squared / cell_count + 1e-06)
        sc_ref[it + 1 : it + 2, :] = scale
        gain = gain / scale
        if it == ITERS - 2:
            sum_probe = jnp.sum(told[:, ITERS, :] * gain * gain, axis=0, keepdims=True)
        gain = gain * told[:, ITERS + 1 + it, :]
    sum_back = jnp.sum(told[:, ITERS - 1, :] * gain * gain, axis=0, keepdims=True)
    sc_ref[0:1, :] = jnp.sqrt(jnp.sqrt(sum_back / sum_probe))
    copyy().wait_recv()
    for q in range(2):
        own_gain = 1.0 / jnp.sqrt(sum_back / cell_count + 1e-06)
        for it in range(ITERS - 1):
            own_gain = own_gain * tab[me, q, ITERS + 1 + it : ITERS + 2 + it, :]
            own_gain = own_gain / sc_ref[it + 1 : it + 2, :]
        both = jnp.concatenate([own_gain] * (ch // 128), axis=1).reshape(1, 1, ch)
        po_ref[q * own_rows : (q + 1) * own_rows] = yh[q].astype(F32) * both

    copy3().wait_recv()
    kg_ref[...] = (h3[...].astype(F32) + r3[...].astype(F32)) * grad_scale

    for k, (v, h) in enumerate(SIDES):
        @pl.when(exists(v, h))
        def _(k=k):
            f_copy(k).wait_send()

    for k in range(5):
        p_copy(k).wait_send()
    copya().wait_send()
    copyy().wait_send()
    copy0().wait_send()
    for k in range(1, half):
        copy1(k).wait_send()
    for k in range(1, nr):
        copy2(k).wait_send()
    copy3().wait_send()

    for one in stores:
        one.wait()

    def sent(k, c):
        copyt(k).wait_send()
        return c

    lax.fori_loop(1, n, sent, 0)


def finish(
    o_in, g_in, kg_in, po_in, sc_in, o_out, g_out, kg_out, po_out, lip, trace,
    o_mid, g_mid, kg_mid, po_mid, in_sems, out_sems,
):
    parts = []
    for a in range(o_in.shape[0]):
        parts.append((o_in.at[a], o_mid.at[a], o_out.at[a]))
        parts.append((g_in.at[a], g_mid.at[a], g_out.at[a]))
    parts.append((po_in, po_mid, po_out))
    parts.append((kg_in, kg_mid, kg_out))
    inward = [
        pltpu.make_async_copy(src, mid, in_sems.at[i]) for i, (src, mid, _) in enumerate(parts)
    ]
    outward = [
        pltpu.make_async_copy(mid, dst, out_sems.at[i]) for i, (_, mid, dst) in enumerate(parts)
    ]
    for one in inward:
        one.start()
    lip[0] = sc_in[0, 0]
    for i in range(ITERS - 1):
        trace[i] = sc_in[i + 1, 0]
    for one, two in zip(inward, outward):
        one.wait()
        two.start()
    for two in outward:
        two.wait()


def solution(mesh):
    nr, nc = mesh.shape["rows"], mesh.shape["cols"]
    reps = mesh.shape["rep"]

    def per_device(inputs, upstream, weights, probe_init):
        batch, height, breadth, ch = inputs.shape
        n = nr * nc
        half = nc // 2
        dper = ch // n
        halo = 2 * ITERS
        wide = breadth + 2 * halo
        cell_count = float(height * nr * breadth * nc * ch)
        grad_scale = 1.0 / math.sqrt(batch * reps * height * nr * breadth * nc)
        cells = height * breadth
        sem = pltpu.SemaphoreType.DMA
        vmem = pl.BlockSpec(memory_space=pltpu.VMEM)
        scratch = [
            ((2, 2 * batch, breadth, ch), BF16),
            ((2, 2 * batch, breadth, ch), BF16),
            ((2, 2 * batch, height, ch), BF16),
            ((2, 2 * batch, height, ch), BF16),
            ((2, 2, 2 * batch, 16, ch), BF16),
            ((2, 2, 2 * batch, 16, ch), BF16),
            ((height, breadth, ch), BF16),
            ((halo, breadth, ch), BF16),
            ((2, height * halo // 16, 16, ch), BF16),
            ((2, height * halo // 16, 16, ch), BF16),
            ((2, halo * halo // 16, 16, ch), BF16),
            ((2, halo * halo // 16, 16, ch), BF16),
            ((batch, height + 2, breadth, 3 * ch), BF16),
            ((batch, height + 2, breadth, 3 * ch), BF16),
            ((height + halo, wide, 3 * ch), BF16),
            ((height + halo, wide, 3 * ch), BF16),
            ((3, 3 * ch, ch), BF16),
            ((ch, batch * cells), BF16),
            ((2, half, nr, dper, 9 * ch), BF16),
            ((half, nr, dper, 9 * ch), BF16),
            ((half, nr, dper, 9 * ch), BF16),
            ((half - 1, nr, dper, 9 * ch), BF16),
            ((nr, dper, 9 * ch), BF16),
            ((nr - 1, dper, 9 * ch), BF16),
            ((dper, 9 * ch), BF16),
            ((dper, 9 * ch), BF16),
            ((n, 2, 8, 128), F32),
            ((2, height // 2, breadth, ch), BF16),
        ]
        anywhere = pl.BlockSpec(memory_space=pl.ANY)
        staged = [
            (inputs.shape, BF16), (inputs.shape, BF16), (weights.shape, BF16),
            (probe_init.shape, F32), (inputs.shape, BF16), (inputs.shape, BF16),
        ]
        outs = pl.pallas_call(
            functools.partial(kernel, nr, nc, (cell_count, grad_scale)),
            out_shape=(
                jax.ShapeDtypeStruct(inputs.shape, BF16),
                jax.ShapeDtypeStruct(inputs.shape, BF16),
                jax.ShapeDtypeStruct((dper, 9 * ch), F32),
                jax.ShapeDtypeStruct(probe_init.shape, F32),
                jax.ShapeDtypeStruct((8, 128), F32),
            ),
            in_specs=[anywhere] * 4,
            out_specs=[anywhere] * 2 + [vmem] * 3,
            scratch_shapes=[pltpu.VMEM(s, t) for s, t in staged]
            + [sem((4,)), sem((2,))]
            + [pltpu.VMEM(s, t) for s, t in scratch]
            + [
                sem((8,)), sem((8,)), sem((5,)), sem((5,)), sem((2,)),
                sem((max(half - 1, 1),)), sem((max(half - 1, 1),)),
                sem((nr - 1,)), sem((nr - 1,)), sem((2,)), sem((n,)), sem((n,)),
                sem((2,)), sem((2,)),
            ],
            compiler_params=pltpu.CompilerParams(
                collective_id=0, has_side_effects=True, vmem_limit_bytes=60 * 2**20
            ),
        )(inputs, upstream, weights, probe_init)
        smem = pl.BlockSpec(memory_space=pltpu.SMEM)
        *arrays, lipschitz, norm_trace = pl.pallas_call(
            finish,
            out_shape=tuple(jax.ShapeDtypeStruct(x.shape, x.dtype) for x in outs[:4])
            + (jax.ShapeDtypeStruct((1,), F32), jax.ShapeDtypeStruct((ITERS - 1,), F32)),
            in_specs=[anywhere] * 4 + [smem],
            out_specs=[anywhere] * 4 + [smem] * 2,
            scratch_shapes=[pltpu.VMEM(x.shape, x.dtype) for x in outs[:4]]
            + [sem((2 * batch + 2,)), sem((2 * batch + 2,))],
            compiler_params=pltpu.CompilerParams(vmem_limit_bytes=60 * 2**20),
        )(*outs)
        return (*arrays, lipschitz.reshape(()), norm_trace)

    placed = (
        P("rep", "rows", "cols", None),
        P("rep", "rows", "cols", None),
        P(),
        P("rows", "cols", None),
    )
    return jax.shard_map(
        per_device,
        mesh=mesh,
        in_specs=placed,
        out_specs=(
            P("rep", "rows", "cols", None),
            P("rep", "rows", "cols", None),
            P(("rows", "cols"), None),
            P("rows", "cols", None),
            P(),
            P(),
        ),
        check_vma=False,
    )
```
